128 devices in a mesh: side: 2 (over y_hi), grp: 32 (over x, z, y_lo), tp: 2 (over core).
Axes of the slice: x: 4, y: 4 (y_hi: 2, y_lo: 2; y = y_hi * 2 + y_lo), z: 4, core: 2. Of those that a mesh axis runs over, the one named last changes fastest.
Arguments:
- residual: bfloat16 [2, 512, 7168], P('side', 'grp'), may hold values from -14 to 14
- moe_gain: bfloat16 [2, 7168], P('side'), may hold values from 0.5 to 1.5
- router: bfloat16 [2, 16, 7168], P('side'), may hold values from -0.0625 to 0.0625
- routes: int32 [2, 512, 8], P('side', 'grp'), may hold values from 0 to 15, all different within a row; in each aligned block of 8 rows (0 to 7, 8 to 15, ..., all dimensions but the last counted through in order) at most 5 rows name the same one
- gate_w: bfloat16 [2, 7168, 16384], P('side', None, ('grp', 'tp')), may hold values from -0.0625 to 0.0625
- up_w: bfloat16 [2, 7168, 16384], P('side', None, ('grp', 'tp')), may hold values from -0.0625 to 0.0625
- down_w: bfloat16 [2, 16384, 7168], P('side', ('grp', 'tp')), may hold values from -0.1875 to 0.1875
- attn_gain: bfloat16 [2, 7168], P('side', 'tp'), may hold values from 0.5 to 1.5
- kv_proj: bfloat16 [2, 576, 7168], P('side', None, 'tp'), may hold values from -0.0625 to 0.0625
- kv_gain: bfloat16 [2, 512], P('side'), may hold values from 0.5 to 1.5
- cache_latent: bfloat16 [2, 512, 128, 512], P('side', 'grp'), may hold values from -5 to 5
- cache_rope: bfloat16 [2, 512, 64, 128], P('side', 'grp'), may hold values from -5 to 5
- lengths: int32 [2, 512], P('side', 'grp'), may hold values from 2 to 128, as said below
- query_latent: bfloat16 [2, 512, 64, 512], P('side', 'grp', 'tp'), may hold values from -34 to 34
- query_rope: bfloat16 [2, 512, 4096], P('side', 'grp', 'tp'), may hold values from -5 to 5
Outputs:
- resid_out: bfloat16 [2, 512, 7168], P('side', 'grp')
- new_latent: bfloat16 [2, 512, 512], P('side', 'grp')
- new_rope: bfloat16 [2, 512, 64], P('side', 'grp')
- attn_latent: bfloat16 [2, 512, 64, 512], P('side', 'grp', 'tp')
The draws below stay inside these ranges and needn't reach their ends.
Inputs may be any that keep to these rules, and one draw needn't show every extreme that they name: `routes`: within each aligned block of 8 rows every row names 8 different experts and no expert is named by more than 5 rows of the block. `lengths`: every attention group's 16 sequences include one with exactly 128 cached tokens.
All inputs are finite; a program needn't handle non-finite values.
Results may differ from the reference program's by a relative error of at most 0.015.
Values may be sent and summed in bfloat16 or wider, within the bound.
No kernel may reach another device: no remote copies, remote signals or barrier semaphores. Data moves between devices by JAX's collectives and lax.ppermute only.
A program may use at most 128 MiB of HBM per device.

```python
import math
import jax
import jax.numpy as jnp
import numpy as np
from jax import lax

D = 7168
LAT = 512
ROPE = 64
HEADS = 64
FFW = 1024
EXPERTS = 16
TOP = 8
MB = 8
LMAX = 128
TOK = 16
TOKENS = 512
CAP = 5
KVW = 576
FF_DEV = 256


def cache_core(key):
    return jax.random.normal(key, (2, TOKENS, LMAX, LAT), jnp.float32)


def draw_cache_latent(key, part):
    raw_draw = cache_core(key)
    return jnp.clip(raw_draw, -5.0, 5.0).astype(jnp.bfloat16)


def draw_query_latent(key, part):
    key = jax.random.fold_in(key, 5)
    first_key = jax.random.fold_in(key, 0)
    raw_draw = jax.random.normal(first_key, (2, TOKENS, HEADS, LAT), jnp.float32)
    return jnp.clip(raw_draw, -5.0, 5.0).astype(jnp.bfloat16)


def draw_residual(key, part):
    key = jax.random.fold_in(key, 1)
    first_key = jax.random.fold_in(key, 0)
    raw_draw = jax.random.normal(first_key, (2, TOKENS, D), jnp.float32)
    column_pos = jnp.arange(D, dtype=jnp.float32) / D
    rising = 3.0 ** column_pos
    return (0.6 * jnp.clip(raw_draw, -4.5, 4.5) * rising).astype(jnp.bfloat16)


def draw_lengths(key, part):
    key = jax.random.fold_in(key, 7)
    drawn_lengths = jax.random.randint(key, (2, TOKENS), 2, LMAX + 1, jnp.int32)
    positions = jnp.arange(TOKENS, dtype=jnp.int32)
    longest = positions % TOK == positions // TOK * 5 % TOK
    return jnp.where(longest[None, :], LMAX, drawn_lengths).astype(jnp.int32)


def block_levels(rng, dims, pieces, least, largest):
    def one(axis_at, blocks):
        steps = jax.random.uniform(jax.random.fold_in(jax.random.fold_in(rng, 6), axis_at), (blocks,), jnp.float32, least / len(pieces), largest / len(pieces))
        return jnp.repeat(jnp.exp(steps), dims[axis_at] // blocks).reshape((-1,) + (1,) * (len(dims) - axis_at - 1))

    level = one(*pieces[0])
    for cut in pieces[1:]:
        level = level * one(*cut)
    return level


def assign_block(key, own, number, rows, amount, top, most, slope):
    sequence = jax.random.permutation(key, amount)
    packed, common = shares(amount, rows * top, most, slope, True), shares(amount, rows * top, most, slope, False)
    places = jnp.arange(amount)

    def named(sizes, turn):
        used = int((sizes > 0).sum())
        fixed = max(1, used // 4)
        shifted = fixed + (places - fixed + turn * (used - fixed)) % max(1, amount - fixed)
        return jnp.zeros((amount,), jnp.int32).at[sequence[jnp.where(places < fixed, places, shifted)]].set(jnp.asarray(sizes, jnp.int32))

    sizes = jnp.where(number % 4 == 0, named(packed, number // 4), named(common, number - number // 4 - 1))
    mixed = jax.random.permutation(jax.random.fold_in(own, 3), amount)
    source_of, sink = mixed[0:amount // 2 * 2:2], mixed[1:amount // 2 * 2:2]
    room = jnp.minimum(sizes[source_of] - 1, most - sizes[sink]) // 2
    room = jnp.where((source_of == sequence[0]) | (sink == sequence[0]) | (sizes[sink] == 0), 0, jnp.maximum(room, 0))
    shifted = jax.random.randint(jax.random.fold_in(own, 4), (amount // 2,), 0, 1 << 20) % (room + 1)
    sizes = sizes.at[source_of].add(-shifted).at[sink].add(shifted)
    members = jnp.searchsorted(jnp.cumsum(sizes), jnp.arange(rows * top), side="right").astype(jnp.int32)
    grid = members.reshape(top, rows).T
    grid = grid[jax.random.permutation(jax.random.fold_in(own, 1), rows)]
    turn = jax.random.randint(jax.random.fold_in(own, 2), (rows, 1), 0, top)
    return jnp.take_along_axis(grid, (jnp.arange(top)[None, :] + turn) % top, axis=1)


def shares(number_of, total, limit, slope, full):
    portions = [(1 << 20) // math.isqrt(standing ** slope) + 1 for standing in range(1, number_of + 1)]
    largest = limit if full else min(limit, max(-(-total // number_of), total * portions[0] // sum(portions)))
    least = 1 if total - largest >= number_of - 1 else 0
    given, surplus = [largest] + [least] * (number_of - 1), total - largest - least * (number_of - 1)
    while surplus > 0:
        free = [i for i in range(1, number_of) if given[i] < largest] or [i for i in range(1, number_of) if given[i] < limit]
        mass, remaining = sum([portions[i] for i in free]), surplus
        for i in free:
            addition = min(limit - given[i], max(1, remaining * portions[i] // mass), surplus)
            given[i] = given[i] + addition
            surplus = surplus - addition
    return np.array(given)


def scatter_about(key, shape, scale, most, shards=(), kind=jnp.bfloat16):
    factor_of = block_levels(key, shape, shards, -0.22, 0.18) if shards else 1.0
    values = jax.random.normal(key, shape, jnp.float32) * scale * factor_of
    return jnp.minimum(jnp.maximum(values, -most), most).astype(kind)


def setup_inputs(seed: int = 0) -> dict:
    key_list = jax.random.split(jax.random.key(seed), 16)
    residual = draw_residual(jax.random.fold_in(key_list[15], 71), 0)
    moe_gain = jnp.clip(1.0 + 0.1 * jax.random.normal(key_list[1], (2, D), jnp.float32), 0.5, 1.5).astype(jnp.bfloat16)
    router = scatter_about(key_list[2], (2, EXPERTS, D), D ** -0.5, 0.0625, ((0, 2),))
    routes_keys = jax.random.split(jax.random.fold_in(key_list[3], 1), 2 * TOKENS // MB)
    routes_turns = jax.random.permutation(jax.random.fold_in(key_list[3], 3), 2 * TOKENS // MB)
    routes = jax.vmap(lambda own, number: assign_block(jax.random.fold_in(key_list[3], 2), own, number, MB, EXPERTS, TOP, CAP, 2))(routes_keys, routes_turns).reshape((2, TOKENS, TOP))
    gate_w = scatter_about(key_list[4], (2, D, EXPERTS * FFW), D ** -0.5, 0.0625, ((0, 2), (2, 64)))
    up_w = scatter_about(key_list[5], (2, D, EXPERTS * FFW), D ** -0.5, 0.0625, ((0, 2), (2, 64)))
    down_w = scatter_about(key_list[6], (2, EXPERTS * FFW, D), FFW ** -0.5, 0.1875, ((0, 2), (1, 64)))
    attn_gain = jnp.clip(1.0 + 0.1 * jax.random.normal(key_list[7], (2, D), jnp.float32), 0.5, 1.5).astype(jnp.bfloat16)
    kv_proj = scatter_about(key_list[8], (2, KVW, D), D ** -0.5, 0.0625, ((0, 2), (2, 2)))
    kv_gain = jnp.clip(1.0 + 0.1 * jax.random.normal(key_list[9], (2, LAT), jnp.float32), 0.5, 1.5).astype(jnp.bfloat16)
    cache_latent = draw_cache_latent(jax.random.fold_in(key_list[15], 71), 0)
    cache_rope = scatter_about(key_list[11], (2, TOKENS, ROPE, LMAX), 1.0, 5.0, ((0, 2), (1, 32)))
    lengths = draw_lengths(jax.random.fold_in(key_list[15], 71), 0)
    query_latent = draw_query_latent(jax.random.fold_in(key_list[15], 71), 0)
    query_rope = scatter_about(key_list[14], (2, TOKENS, HEADS * ROPE), 1.0, 5.0, ((0, 2), (1, 32), (2, 2)))
    return dict(residual=residual, moe_gain=moe_gain, router=router, routes=routes, gate_w=gate_w, up_w=up_w, down_w=down_w, attn_gain=attn_gain, kv_proj=kv_proj, kv_gain=kv_gain, cache_latent=cache_latent, cache_rope=cache_rope, lengths=lengths, query_latent=query_latent, query_rope=query_rope)


NORM_EPS = 1e-06
ROUTE_SCALE = 2.5
ROPE_BASE = 10000.0
SCORE_SCALE = 192.0 ** (-0.5)
FULL_PRECISION = lax.Precision.HIGHEST

def rms_scale(values):
    return lax.rsqrt(lax.optimization_barrier(jnp.mean(values * values, axis=-1, keepdims=True)) + NORM_EPS)

def rotate(pair_part, position):
    half_width = pair_part.shape[-1] // 2
    step_ids = lax.broadcasted_iota(jnp.int32, (1, half_width), 1).astype(jnp.float32)
    inverse_freq = jnp.exp(-(2.0 * step_ids / pair_part.shape[-1]) * jnp.log(ROPE_BASE))
    angles = position.astype(jnp.float32)[:, None] * inverse_freq
    first_half = pair_part[:, :half_width]
    second_half = pair_part[:, half_width:]
    cosine = jnp.cos(angles)
    sine_part = jnp.sin(angles)
    return jnp.concatenate([first_half * cosine - second_half * sine_part, first_half * sine_part + second_half * cosine], axis=-1)

def expert_outputs(row_block, gate_part, up_part, down_part):
    gate_val = jnp.dot(row_block, gate_part, preferred_element_type=jnp.float32)
    up_val = jnp.dot(row_block, up_part, preferred_element_type=jnp.float32)
    hidden = (jax.nn.silu(gate_val) * up_val).astype(jnp.bfloat16)
    running = jnp.zeros((row_block.shape[0], down_part.shape[1]), jnp.float32)
    for block_idx in range(FFW // FF_DEV):
        start = block_idx * FF_DEV
        piece_out = jnp.dot(hidden[:, start:start + FF_DEV], down_part[start:start + FF_DEV], preferred_element_type=jnp.float32).astype(jnp.bfloat16)
        running = running + lax.optimization_barrier(piece_out).astype(jnp.float32)
    return running

def reference(residual, moe_gain, router, routes, gate_w, up_w, down_w, attn_gain, kv_proj, kv_gain, cache_latent, cache_rope, lengths, query_latent, query_rope):
    x_rows = residual[0].astype(jnp.float32)
    normed = x_rows * rms_scale(x_rows) * moe_gain[0].astype(jnp.float32)
    logits = jnp.dot(normed, router[0].astype(jnp.float32).T, precision=FULL_PRECISION)
    moe_in = normed.astype(jnp.bfloat16)
    scores = jax.nn.sigmoid(logits)
    chosen = routes[0]
    picked = jnp.take_along_axis(scores, chosen, axis=1)
    weight = (ROUTE_SCALE * picked / lax.optimization_barrier(jnp.sum(picked, axis=1, keepdims=True))).astype(jnp.bfloat16)
    blocks = TOKENS // MB
    matches = (chosen[:, :, None] == jnp.arange(EXPERTS, dtype=jnp.int32)[None, None, :]).astype(jnp.int32)
    per_row = lax.optimization_barrier(jnp.sum(matches, axis=1)).astype(jnp.int32).reshape(blocks, MB, EXPERTS)
    before = (jnp.cumsum(per_row, axis=1).astype(jnp.int32) - per_row).reshape(TOKENS, EXPERTS)
    slots = lax.optimization_barrier(jnp.sum(matches * before[:, None, :], axis=2)).astype(jnp.int32)
    block_of = jnp.broadcast_to((jnp.arange(TOKENS, dtype=jnp.int32) // MB)[:, None], chosen.shape).astype(jnp.int32)
    values = jnp.broadcast_to(moe_in[:, None, :], (TOKENS, TOP, D))
    buffer = jnp.zeros((EXPERTS, blocks, CAP, D), jnp.bfloat16).at[chosen, block_of, slots].set(values)
    gate_all = gate_w[1].reshape(D, EXPERTS, FFW).transpose(1, 0, 2)
    up_all = up_w[1].reshape(D, EXPERTS, FFW).transpose(1, 0, 2)
    down_all = down_w[1].reshape(EXPERTS, FFW, D)

    def serve_expert(operands):
        row_block, gate_part, up_part, down_part = operands
        return expert_outputs(row_block.reshape(blocks * CAP, D), gate_part, up_part, down_part).reshape(blocks, CAP, D)
    served = lax.map(serve_expert, (buffer, gate_all, up_all, down_all))
    gathered = served[chosen, block_of, slots]
    moe_out = lax.optimization_barrier(jnp.sum(weight.astype(jnp.float32)[:, :, None] * gathered, axis=1))
    updated = (x_rows + moe_out).astype(jnp.bfloat16)
    updated_f = updated.astype(jnp.float32)
    scaled = (updated_f * attn_gain[0].astype(jnp.float32)).astype(jnp.bfloat16)
    kv_raw = jnp.dot(scaled, kv_proj[0].T, preferred_element_type=jnp.float32) * rms_scale(updated_f)
    latent = kv_raw[:, :LAT]
    fresh_lat = (latent * rms_scale(latent) * kv_gain[0].astype(jnp.float32)).astype(jnp.bfloat16)
    fresh_rot = rotate(kv_raw[:, LAT:], lengths[0]).astype(jnp.bfloat16)
    query_f = query_latent[0].astype(jnp.float32)
    query_r = query_rope[0].reshape(TOKENS, HEADS, ROPE).astype(jnp.float32)
    cache_f = cache_latent[0].astype(jnp.float32)
    cache_r = cache_rope[0].astype(jnp.float32)
    fresh_lat_f = fresh_lat.astype(jnp.float32)
    fresh_rot_f = fresh_rot.astype(jnp.float32)
    cache_scores = (jnp.einsum('thl,tpl->thp', query_f, cache_f, precision=FULL_PRECISION) + jnp.einsum('thr,trp->thp', query_r, cache_r, precision=FULL_PRECISION)) * SCORE_SCALE
    own_scores = (jnp.einsum('thl,tl->th', query_f, fresh_lat_f, precision=FULL_PRECISION) + jnp.einsum('thr,tr->th', query_r, fresh_rot_f, precision=FULL_PRECISION)) * SCORE_SCALE
    usable = jnp.arange(LMAX, dtype=jnp.int32)[None, None, :] < lengths[0][:, None, None]
    cache_scores = jnp.where(usable, cache_scores, -1e+30)
    peak = jnp.maximum(lax.optimization_barrier(jnp.max(cache_scores, axis=2)), own_scores)
    cache_weights = jnp.where(usable, jnp.exp(cache_scores - peak[:, :, None]), 0.0)
    own_weight = jnp.exp(own_scores - peak)
    denominator = lax.optimization_barrier(jnp.sum(cache_weights, axis=2)) + own_weight
    cache_probs = (cache_weights / denominator[:, :, None]).astype(jnp.bfloat16)
    own_probs = (own_weight / denominator).astype(jnp.bfloat16)
    mixed = jnp.einsum('thp,tpl->thl', cache_probs.astype(jnp.float32), cache_f, precision=FULL_PRECISION)
    mixed = mixed + own_probs.astype(jnp.float32)[:, :, None] * fresh_lat_f[:, None, :]
    attended = mixed.astype(jnp.bfloat16)
    return (jnp.stack([updated, jnp.zeros_like(updated)]), jnp.stack([fresh_lat, jnp.zeros_like(fresh_lat)]), jnp.stack([fresh_rot, jnp.zeros_like(fresh_rot)]), jnp.stack([attended, jnp.zeros_like(attended)]))
```

```python
import jax
import jax.numpy as jnp
from jax import lax
from jax.sharding import PartitionSpec as P

SIDES = 2
NX = 4
NZ = 4
NY = 2
NT = 2
AXES = ("side", "grp", "tp")

NORM_EPS = 1e-06
ROUTE_SCALE = 2.5
ROPE_BASE = 10000.0
SCORE_SCALE = 192.0 ** (-0.5)
WEIGHT_LANES = 128

BF16 = jnp.bfloat16
F32 = jnp.float32


def place(side, x, z, y, t):
    return side * (NX * NZ * NY * NT) + ((x * NZ + z) * NY + y) * NT + t


def columns():
    return [(x, z, y, t) for x in range(NX) for z in range(NZ) for y in range(NY) for t in range(NT)]


def cross_pairs(source, flip):
    return [
        (place(source, x, z, y, t), place(1 - source, x, z, (y + flip) % NY, t))
        for x, z, y, t in columns()
    ]


def ring_pairs(leg, step):
    pairs = []
    for x, z, y, t in columns():
        along_x = leg == t
        to = ((x + step) % NX, z) if along_x else (x, (z + step) % NZ)
        pairs.append((place(1, x, z, y, t), place(1, to[0], to[1], y, t)))
    return pairs


def core_pairs(side):
    return [(place(side, x, z, y, t), place(side, x, z, y, 1 - t)) for x, z, y, t in columns()]


def send(value, pairs):
    return lax.ppermute(value, AXES, pairs)


def gather_ring(own, leg):
    half = own.shape[0] // 2
    before = send(own, ring_pairs(leg, 1))
    after = send(own, ring_pairs(leg, -1))
    far_a = send(before[:half], ring_pairs(leg, 1))
    far_b = send(after[half:], ring_pairs(leg, -1))
    return jnp.concatenate([own, before, after, far_a, far_b], axis=0)


def add(*values):
    total = values[0].astype(F32)
    for value in values[1:]:
        total = total + value.astype(F32)
    return total.astype(BF16)


def scatter_ring(parts, leg):
    rows = parts.shape[0] // 4
    half = rows // 2
    own, before, after = (parts[i * rows : (i + 1) * rows] for i in range(3))
    far_a, far_b = parts[3 * rows : 3 * rows + half], parts[3 * rows + half :]
    from_after = send(far_a, ring_pairs(leg, -1))
    from_before = send(far_b, ring_pairs(leg, 1))
    before = jnp.concatenate([add(before[:half], from_after), before[half:]], axis=0)
    after = jnp.concatenate([after[:half], add(after[half:], from_before)], axis=0)
    return add(own, send(before, ring_pairs(leg, -1)), send(after, ring_pairs(leg, 1)))


def rms_scale(values):
    return lax.rsqrt(jnp.mean(values * values, axis=-1, keepdims=True) + NORM_EPS)


def rotate(pair_part, position):
    half_width = pair_part.shape[-1] // 2
    step_ids = lax.broadcasted_iota(jnp.int32, (1, half_width), 1).astype(F32)
    inverse_freq = jnp.exp(-(2.0 * step_ids / pair_part.shape[-1]) * jnp.log(ROPE_BASE))
    angles = position.astype(F32)[:, None] * inverse_freq
    first_half = pair_part[:, :half_width]
    second_half = pair_part[:, half_width:]
    cosine = jnp.cos(angles)
    sine_part = jnp.sin(angles)
    return jnp.concatenate(
        [
            first_half * cosine - second_half * sine_part,
            first_half * sine_part + second_half * cosine,
        ],
        axis=-1,
    )


def attend_cache(operands):
    query_lat, query_rot, cache_lat, cache_rot, seq_lengths = operands
    scores = (
        jnp.einsum("thl,tpl->thp", query_lat, cache_lat, preferred_element_type=F32)
        + jnp.einsum("thr,trp->thp", query_rot, cache_rot, preferred_element_type=F32)
    ) * SCORE_SCALE
    usable = lax.broadcasted_iota(jnp.int32, scores.shape, 2) < seq_lengths[:, None, None]
    scores = jnp.where(usable, scores, -1e30)
    peak = jnp.max(scores, axis=2)
    weights = jnp.where(usable, jnp.exp(scores - peak[:, :, None]), 0.0)
    mixed = jnp.einsum("thp,tpl->thl", weights.astype(BF16), cache_lat, preferred_element_type=F32)
    return mixed, peak, jnp.sum(weights, axis=2)


def body(
    residual,
    moe_gain,
    router,
    routes,
    gate_w,
    up_w,
    down_w,
    attn_gain,
    kv_proj,
    kv_gain,
    cache_latent,
    cache_rope,
    lengths,
    query_latent,
    query_rope,
):
    is_attn = lax.axis_index("side") == 0
    tp_index = lax.axis_index("tp")
    own_expert = lax.axis_index("grp") // NY
    model_width = residual.shape[2]
    group_rows = residual.shape[1]
    rows = group_rows // NT
    experts = router.shape[1]
    half_width = attn_gain.shape[1]
    latent_width = kv_gain.shape[1]
    heads_here = query_latent.shape[2]

    def own_rows(value):
        return lax.dynamic_slice_in_dim(value, tp_index * rows, rows, 0)

    x_rows = own_rows(residual[0]).astype(F32)
    normed = x_rows * rms_scale(x_rows) * moe_gain[0].astype(F32)
    logits = jnp.dot(normed, router[0].astype(F32).T, precision=lax.Precision.HIGHEST)
    scores = jax.nn.sigmoid(logits)
    chosen = own_rows(routes[0])
    expert_iota = lax.broadcasted_iota(jnp.int32, (1, 1, experts), 2)
    named = jnp.any(chosen[:, :, None] == expert_iota, axis=1)
    picked = jnp.where(named, scores, 0.0)
    weight = (ROUTE_SCALE * picked / jnp.sum(picked, axis=1, keepdims=True)).astype(BF16)
    outgoing = jnp.concatenate(
        [normed.astype(BF16), jnp.pad(weight, ((0, 0), (0, WEIGHT_LANES - experts)))], axis=1
    )

    gate_other, up_other, down_other = (
        send(value[0], core_pairs(1)) for value in (gate_w, up_w, down_w)
    )
    kv_other = send(kv_proj[0], core_pairs(0))
    gain_other = send(attn_gain, core_pairs(0))

    arrived = jnp.concatenate(
        [send(outgoing, cross_pairs(0, 0)), send(outgoing, cross_pairs(0, 1))], axis=0
    )
    everything = gather_ring(gather_ring(arrived, 0), 1)
    flat = everything[:, :model_width]
    all_weights = everything[:, model_width : model_width + experts].astype(F32)
    mine = lax.broadcasted_iota(jnp.int32, (1, experts), 1) == own_expert
    row_weight = jnp.sum(jnp.where(mine, all_weights, 0.0), axis=1, keepdims=True)

    def hidden_of(gate_part, up_part):
        gate_val = jnp.dot(flat, gate_part, preferred_element_type=F32)
        up_val = jnp.dot(flat, up_part, preferred_element_type=F32)
        return (jax.nn.silu(gate_val) * up_val).astype(BF16)

    answer = jnp.dot(hidden_of(gate_w[0], up_w[0]), down_w[0], preferred_element_type=F32) + jnp.dot(
        hidden_of(gate_other, up_other), down_other, preferred_element_type=F32
    )
    answer = (answer * row_weight).astype(BF16)
    answer = scatter_ring(scatter_ring(answer, 1), 0)
    back_same = send(answer[:rows], cross_pairs(1, 0))
    back_flip = send(answer[rows:], cross_pairs(1, 1))

    operands = (
        query_latent[0],
        query_rope[0].reshape(group_rows, heads_here, -1),
        cache_latent[0],
        cache_rope[0],
        lengths[0],
    )

    def skip_attention(unused):
        return (
            jnp.zeros((group_rows, heads_here, latent_width), F32),
            jnp.zeros((group_rows, heads_here), F32),
            jnp.ones((group_rows, heads_here), F32),
        )

    mixed, peak, mass = lax.cond(is_attn, attend_cache, skip_attention, operands)

    moe_total = back_same.astype(F32) + back_flip.astype(F32)
    updated = (x_rows + moe_total).astype(BF16)
    updated_other = send(updated, core_pairs(0))
    updated_f = updated.astype(F32)

    def project(start, gain_part, proj_part):
        part = lax.dynamic_slice_in_dim(updated, start, half_width, 1).astype(F32)
        scaled = (part * gain_part.astype(F32)).astype(BF16)
        return lax.dot_general(
            scaled, proj_part, (((1,), (1,)), ((), ())), preferred_element_type=F32
        )

    kv_raw = project(tp_index * half_width, attn_gain[0], kv_proj[0]) + project(
        (1 - tp_index) * half_width, gain_other[0], kv_other
    )
    kv_raw = kv_raw * rms_scale(updated_f)
    latent = kv_raw[:, :latent_width]
    fresh_lat = (latent * rms_scale(latent) * kv_gain[0].astype(F32)).astype(BF16)
    fresh_rot = rotate(kv_raw[:, latent_width:], own_rows(lengths[0])).astype(BF16)
    fresh = jnp.concatenate([fresh_lat, fresh_rot], axis=1)
    fresh_other = send(fresh, core_pairs(0))

    def both(own, other):
        first = tp_index == 0
        return jnp.concatenate([jnp.where(first, own, other), jnp.where(first, other, own)], axis=0)

    fresh = both(fresh, fresh_other)
    fresh_lat, fresh_rot = fresh[:, :latent_width], fresh[:, latent_width:]
    own_scores = (
        jnp.sum(query_latent[0].astype(F32) * fresh_lat.astype(F32)[:, None, :], axis=2)
        + jnp.sum(operands[1].astype(F32) * fresh_rot.astype(F32)[:, None, :], axis=2)
    ) * SCORE_SCALE
    top = jnp.maximum(peak, own_scores)
    kept = jnp.exp(peak - top)
    own_weight = jnp.exp(own_scores - top)
    denominator = mass * kept + own_weight
    attended = (
        mixed * (kept / denominator)[:, :, None]
        + (own_weight / denominator)[:, :, None] * fresh_lat.astype(F32)[:, None, :]
    ).astype(BF16)

    def keep_role(value):
        return jnp.where(is_attn, value, jnp.zeros_like(value))[None]

    return (
        keep_role(both(updated, updated_other)),
        keep_role(fresh_lat),
        keep_role(fresh_rot),
        keep_role(attended),
    )


def solution(mesh):
    in_specs = (
        P("side", "grp", None),
        P("side", None),
        P("side", None, None),
        P("side", "grp", None),
        P("side", None, ("grp", "tp")),
        P("side", None, ("grp", "tp")),
        P("side", ("grp", "tp"), None),
        P("side", "tp"),
        P("side", None, "tp"),
        P("side", None),
        P("side", "grp", None, None),
        P("side", "grp", None, None),
        P("side", "grp"),
        P("side", "grp", "tp", None),
        P("side", "grp", "tp"),
    )
    out_specs = (
        P("side", "grp", None),
        P("side", "grp", None),
        P("side", "grp", None),
        P("side", "grp", "tp", None),
    )
    return jax.shard_map(body, mesh=mesh, in_specs=in_specs, out_specs=out_specs, check_vma=False)
```

```python
import functools

import jax
import jax.numpy as jnp
from jax import lax
from jax.experimental import pallas as pl
from jax.experimental.pallas import tpu as pltpu
from jax.sharding import PartitionSpec as P

NX = 4
NZ = 4
NY = 2
AXES = ("side", "grp", "tp")

NORM_EPS = 1e-06
ROUTE_SCALE = 2.5
ROPE_BASE = 10000.0
SCORE_SCALE = 192.0 ** (-0.5)
WEIGHT_LANES = 128
CHUNK = 1792

BF16 = jnp.bfloat16
F32 = jnp.float32


def pairs_of(partner):
    cells = [
        (side, x, z, y, t)
        for side in range(2)
        for x in range(NX)
        for z in range(NZ)
        for y in range(NY)
        for t in range(2)
    ]

    def place(cell):
        side, x, z, y, t = cell
        return (((side * NX + x) * NZ + z) * NY + y) * 2 + t

    return [(place(cell), place(partner(*cell))) for cell in cells]


def send(value, partner):
    return lax.ppermute(value, AXES, pairs_of(partner))


def across(flip):
    return lambda side, x, z, y, t: (1 - side, x, z, y ^ flip, t)


def other_core(side, x, z, y, t):
    return side, x, z, y, 1 - t


def ring(leg, flip):
    def partner(side, x, z, y, t):
        return (side, x ^ flip, z, y, t) if leg == t else (side, x, z ^ flip, y, t)

    return partner


def gather_ring(own, leg):
    half = own.shape[0] // 2
    one = send(own, ring(leg, 1))
    three = send(own, ring(leg, 3))
    far_a = send(one[:half], ring(leg, 3))
    far_b = send(three[half:], ring(leg, 1))
    return own, one, three, far_a, far_b


def add(*values):
    total = values[0].astype(F32)
    for value in values[1:]:
        total = total + value.astype(F32)
    return total.astype(BF16)


def scatter_ring(pieces, leg):
    own, one, three, far_a, far_b = pieces
    half = own.shape[0] // 2
    late_a = send(far_a, ring(leg, 3))
    late_b = send(far_b, ring(leg, 1))
    one = jnp.concatenate([add(one[:half], late_a), one[half:]], axis=0)
    three = jnp.concatenate([three[:half], add(three[half:], late_b)], axis=0)
    return add(own, send(one, ring(leg, 1)), send(three, ring(leg, 3)))


def cut(value):
    rows = value.shape[0] // 4
    half = rows // 2
    return (
        value[:rows],
        value[rows : 2 * rows],
        value[2 * rows : 3 * rows],
        value[3 * rows : 3 * rows + half],
        value[3 * rows + half :],
    )


def expert_kernel(steps, expert_ref, *refs):
    pieces, tails = refs[0:5], refs[5:10]
    gate_a, gate_b, up_a, up_b, down_a, down_b = refs[10:16]
    outs = refs[16:21]
    gate_acc, up_acc, hidden, scale = refs[21:25]
    step = pl.program_id(0)
    width = gate_a.shape[1]

    def dot(left, right):
        return jnp.dot(left, right, preferred_element_type=F32)

    @pl.when(step == 0)
    def _():
        gate_acc[...] = jnp.zeros_like(gate_acc)
        up_acc[...] = jnp.zeros_like(up_acc)
        lanes = jnp.concatenate([tail[...] for tail in tails], axis=0).astype(F32)
        mine = lax.broadcasted_iota(jnp.int32, lanes.shape, 1) == expert_ref[0]
        scale[...] = jnp.sum(jnp.where(mine, lanes, 0.0), axis=1, keepdims=True)

    @pl.when(step < steps)
    def _():
        rows = jnp.concatenate([piece[...] for piece in pieces], axis=0)
        gate_acc[:, :width] += dot(rows, gate_a[...])
        gate_acc[:, width:] += dot(rows, gate_b[...])
        up_acc[:, :width] += dot(rows, up_a[...])
        up_acc[:, width:] += dot(rows, up_b[...])

    @pl.when(step == steps - 1)
    def _():
        gate = gate_acc[...]
        hidden[...] = (gate / (1.0 + jnp.exp(-gate)) * up_acc[...]).astype(BF16)

    @pl.when(step >= steps)
    def _():
        answer = dot(hidden[:, :width], down_a[...]) + dot(hidden[:, width:], down_b[...])
        answer = (answer * scale[...]).astype(BF16)
        at = 0
        for out in outs:
            out[...] = answer[at : at + out.shape[0]]
            at += out.shape[0]


def experts(own_expert, pieces, gate_a, gate_b, up_a, up_b, down_a, down_b):
    model_width, width = gate_a.shape
    steps = model_width // CHUNK
    total = sum(piece.shape[0] for piece in pieces)

    def early(step, expert):
        return jnp.minimum(step, steps - 1)

    def late(step, expert):
        return jnp.maximum(step - steps, 0)

    piece_specs = [
        pl.BlockSpec((piece.shape[0], CHUNK), lambda i, e: (0, early(i, e))) for piece in pieces
    ]
    tail_specs = [
        pl.BlockSpec((piece.shape[0], WEIGHT_LANES), lambda i, e: (0, model_width // WEIGHT_LANES))
        for piece in pieces
    ]
    in_specs = [pl.BlockSpec((CHUNK, width), lambda i, e: (early(i, e), 0))] * 4
    down_specs = [pl.BlockSpec((width, CHUNK), lambda i, e: (0, late(i, e)))] * 2
    return pl.pallas_call(
        functools.partial(expert_kernel, steps),
        out_shape=[jax.ShapeDtypeStruct((piece.shape[0], model_width), BF16) for piece in pieces],
        grid_spec=pltpu.PrefetchScalarGridSpec(
            num_scalar_prefetch=1,
            grid=(2 * steps,),
            in_specs=piece_specs + tail_specs + in_specs + down_specs,
            out_specs=[
                pl.BlockSpec((piece.shape[0], CHUNK), lambda i, e: (0, late(i, e)))
                for piece in pieces
            ],
            scratch_shapes=[
                pltpu.VMEM((total, 2 * width), F32),
                pltpu.VMEM((total, 2 * width), F32),
                pltpu.VMEM((total, 2 * width), BF16),
                pltpu.VMEM((total, 1), F32),
            ],
        ),
        compiler_params=pltpu.CompilerParams(vmem_limit_bytes=24 * 1024 * 1024),
        cost_estimate=pl.CostEstimate(
            flops=12 * total * model_width * width,
            bytes_accessed=12 * model_width * width + 4 * total * model_width,
            transcendentals=2 * total * width,
        ),
    )(own_expert, *pieces, *pieces, gate_a, gate_b, up_a, up_b, down_a, down_b)


def rms_scale(values):
    return lax.rsqrt(jnp.mean(values * values, axis=-1, keepdims=True) + NORM_EPS)


def rotate(pair_part, position):
    half_width = pair_part.shape[-1] // 2
    step_ids = lax.broadcasted_iota(jnp.int32, (1, half_width), 1).astype(F32)
    inverse_freq = jnp.exp(-(2.0 * step_ids / pair_part.shape[-1]) * jnp.log(ROPE_BASE))
    angles = position.astype(F32)[:, None] * inverse_freq
    first_half = pair_part[:, :half_width]
    second_half = pair_part[:, half_width:]
    cosine = jnp.cos(angles)
    sine_part = jnp.sin(angles)
    return jnp.concatenate(
        [
            first_half * cosine - second_half * sine_part,
            first_half * sine_part + second_half * cosine,
        ],
        axis=-1,
    )


def attend_cache(operands):
    query_lat, query_rot, cache_lat, cache_rot, seq_lengths = operands
    scores = (
        jnp.einsum("thl,tpl->thp", query_lat, cache_lat, preferred_element_type=F32)
        + jnp.einsum("thr,trp->thp", query_rot, cache_rot, preferred_element_type=F32)
    ) * SCORE_SCALE
    usable = lax.broadcasted_iota(jnp.int32, scores.shape, 2) < seq_lengths[:, None, None]
    scores = jnp.where(usable, scores, -1e30)
    peak = jnp.max(scores, axis=2)
    weights = jnp.where(usable, jnp.exp(scores - peak[:, :, None]), 0.0)
    mixed = jnp.einsum("thp,tpl->thl", weights.astype(BF16), cache_lat, preferred_element_type=F32)
    return mixed, peak, jnp.sum(weights, axis=2)


def body(
    residual,
    moe_gain,
    router,
    routes,
    gate_w,
    up_w,
    down_w,
    attn_gain,
    kv_proj,
    kv_gain,
    cache_latent,
    cache_rope,
    lengths,
    query_latent,
    query_rope,
):
    is_attn = lax.axis_index("side") == 0
    tp_index = lax.axis_index("tp")
    own_expert = (lax.axis_index("grp") // NY).astype(jnp.int32).reshape(1)
    model_width = residual.shape[2]
    group_rows = residual.shape[1]
    rows = group_rows // 2
    half_width = attn_gain.shape[1]
    latent_width = kv_gain.shape[1]
    heads_here = query_latent.shape[2]
    barrier = lax.optimization_barrier

    def own_rows(value):
        return lax.dynamic_slice_in_dim(value, tp_index * rows, rows, 0)

    gate_other, up_other, down_other = (
        send(value[0], other_core) for value in (gate_w, up_w, down_w)
    )
    kv_other = send(kv_proj[0], other_core)
    gain_other = send(attn_gain, other_core)

    x_rows = own_rows(residual[0]).astype(F32)
    normed = x_rows * rms_scale(x_rows) * moe_gain[0].astype(F32)
    logits = jnp.dot(normed, router[0].astype(F32).T, precision=lax.Precision.HIGHEST)
    scores = jax.nn.sigmoid(logits)
    chosen = own_rows(routes[0])
    expert_iota = lax.broadcasted_iota(jnp.int32, (1, 1, router.shape[1]), 2)
    named = jnp.any(chosen[:, :, None] == expert_iota, axis=1)
    picked = jnp.where(named, scores, 0.0)
    weight = (ROUTE_SCALE * picked / jnp.sum(picked, axis=1, keepdims=True)).astype(BF16)
    outgoing = jnp.concatenate(
        [normed.astype(BF16), jnp.pad(weight, ((0, 0), (0, WEIGHT_LANES - weight.shape[1])))],
        axis=1,
    )

    arrived = jnp.concatenate([send(outgoing, across(0)), send(outgoing, across(1))], axis=0)
    arrived, gate_other, up_other = barrier((arrived, gate_other, up_other))
    column = jnp.concatenate(gather_ring(arrived, 0), axis=0)
    column, down_other, kv_other, gain_other = barrier((column, down_other, kv_other, gain_other))
    pieces = gather_ring(column, 1)

    operands = (
        query_latent[0],
        query_rope[0].reshape(group_rows, heads_here, -1),
        cache_latent[0],
        cache_rope[0],
        lengths[0],
    )

    def attention_role(operands, pieces, weights):
        return attend_cache(operands), tuple(
            jnp.zeros((piece.shape[0], model_width), BF16) for piece in pieces
        )

    def expert_role(operands, pieces, weights):
        idle = (
            jnp.zeros((group_rows, heads_here, latent_width), F32),
            jnp.zeros((group_rows, heads_here), F32),
            jnp.ones((group_rows, heads_here), F32),
        )
        return idle, tuple(experts(own_expert, pieces, *weights))

    (mixed, peak, mass), answers = lax.cond(
        is_attn,
        attention_role,
        expert_role,
        operands,
        pieces,
        (gate_w[0], gate_other, up_w[0], up_other, down_w[0], down_other),
    )
    answer = scatter_ring(cut(scatter_ring(answers, 1)), 0)
    back_same = send(answer[:rows], across(0))
    back_flip = send(answer[rows:], across(1))

    moe_total = back_same.astype(F32) + back_flip.astype(F32)
    updated = (x_rows + moe_total).astype(BF16)
    updated_other = send(updated, other_core)
    updated_f = updated.astype(F32)

    def project(start, gain_part, proj_part):
        part = lax.dynamic_slice_in_dim(updated, start, half_width, 1).astype(F32)
        scaled = (part * gain_part.astype(F32)).astype(BF16)
        return lax.dot_general(
            scaled, proj_part, (((1,), (1,)), ((), ())), preferred_element_type=F32
        )

    kv_raw = project(tp_index * half_width, attn_gain[0], kv_proj[0]) + project(
        (1 - tp_index) * half_width, gain_other[0], kv_other
    )
    kv_raw = kv_raw * rms_scale(updated_f)
    latent = kv_raw[:, :latent_width]
    fresh_lat = (latent * rms_scale(latent) * kv_gain[0].astype(F32)).astype(BF16)
    fresh_rot = rotate(kv_raw[:, latent_width:], own_rows(lengths[0])).astype(BF16)
    fresh = jnp.concatenate([fresh_lat, fresh_rot], axis=1)
    fresh_other = send(fresh, other_core)

    def both(own, other):
        first = tp_index == 0
        return jnp.concatenate([jnp.where(first, own, other), jnp.where(first, other, own)], axis=0)

    fresh = both(fresh, fresh_other)
    fresh_lat, fresh_rot = fresh[:, :latent_width], fresh[:, latent_width:]
    own_scores = (
        jnp.sum(query_latent[0].astype(F32) * fresh_lat.astype(F32)[:, None, :], axis=2)
        + jnp.sum(operands[1].astype(F32) * fresh_rot.astype(F32)[:, None, :], axis=2)
    ) * SCORE_SCALE
    top = jnp.maximum(peak, own_scores)
    kept = jnp.exp(peak - top)
    own_weight = jnp.exp(own_scores - top)
    denominator = mass * kept + own_weight
    attended = (
        mixed * (kept / denominator)[:, :, None]
        + (own_weight / denominator)[:, :, None] * fresh_lat.astype(F32)[:, None, :]
    ).astype(BF16)

    def keep_role(value):
        return jnp.where(is_attn, value, jnp.zeros_like(value))[None]

    return (
        keep_role(both(updated, updated_other)),
        keep_role(fresh_lat),
        keep_role(fresh_rot),
        keep_role(attended),
    )


def solution(mesh):
    in_specs = (
        P("side", "grp", None),
        P("side", None),
        P("side", None, None),
        P("side", "grp", None),
        P("side", None, ("grp", "tp")),
        P("side", None, ("grp", "tp")),
        P("side", ("grp", "tp"), None),
        P("side", "tp"),
        P("side", None, "tp"),
        P("side", None),
        P("side", "grp", None, None),
        P("side", "grp", None, None),
        P("side", "grp"),
        P("side", "grp", "tp", None),
        P("side", "grp", "tp"),
    )
    out_specs = (
        P("side", "grp", None),
        P("side", "grp", None),
        P("side", "grp", None),
        P("side", "grp", "tp", None),
    )
    return jax.shard_map(body, mesh=mesh, in_specs=in_specs, out_specs=out_specs, check_vma=False)
```

```python
import functools

import jax
import jax.numpy as jnp
from jax import lax
from jax.experimental import pallas as pl
from jax.experimental.pallas import tpu as pltpu
from jax.sharding import PartitionSpec as P

NX = 4
NZ = 4
NY = 2
AXES = ("side", "grp", "tp")

NORM_EPS = 1e-06
ROUTE_SCALE = 2.5
ROPE_BASE = 10000.0
SCORE_SCALE = 192.0 ** (-0.5)
WEIGHT_LANES = 128
CHUNK = 1792
KERNEL_VMEM = 16 * 1024 * 1024
ROLES_VMEM = 16 * 1024 * 1024
STAGE_VMEM = 1024 * 1024

BF16 = jnp.bfloat16
F32 = jnp.float32


def pairs_of(partner):
    cells = [
        (side, x, z, y, t)
        for side in range(2)
        for x in range(NX)
        for z in range(NZ)
        for y in range(NY)
        for t in range(2)
    ]

    def place(cell):
        side, x, z, y, t = cell
        return (((side * NX + x) * NZ + z) * NY + y) * 2 + t

    return [(place(cell), place(partner(*cell))) for cell in cells]


def send(value, partner):
    return lax.ppermute(value, AXES, pairs_of(partner))


def across(flip):
    return lambda side, x, z, y, t: (1 - side, x, z, y ^ flip, t)


def other_core(side, x, z, y, t):
    return side, x, z, y, 1 - t


def ring(leg, flip):
    def partner(side, x, z, y, t):
        return (side, x ^ flip, z, y, t) if leg == t else (side, x, z ^ flip, y, t)

    return partner


def add(*values):
    total = values[0].astype(F32)
    for value in values[1:]:
        total = total + value.astype(F32)
    return total.astype(BF16)


def gather_ring(first, second, leg, beside=()):
    one_a = send(first, ring(leg, 1))
    three_b = send(second, ring(leg, 3))
    three_a = send(first, ring(leg, 3))
    one_b = send(second, ring(leg, 1))
    one_a, three_b, beside = lax.optimization_barrier((one_a, three_b, beside))
    far_a = send(one_a, ring(leg, 3))
    far_b = send(three_b, ring(leg, 1))
    return first, second, one_a, one_b, three_a, three_b, far_a, far_b, beside


def scatter_ring(pieces, leg):
    first, second, one_a, one_b, three_a, three_b, far_a, far_b = pieces
    late_a = send(far_a, ring(leg, 3))
    late_b = send(far_b, ring(leg, 1))
    from_one_b = send(one_b, ring(leg, 1))
    from_three_a = send(three_a, ring(leg, 3))
    from_one_a = send(add(one_a, late_a), ring(leg, 1))
    from_three_b = send(add(three_b, late_b), ring(leg, 3))
    return add(first, from_one_a, from_three_a), add(second, from_one_b, from_three_b)


def join_pairs(values):
    half = len(values) // 2
    return jnp.concatenate(values[:half], axis=0), jnp.concatenate(values[half:], axis=0)


def split_pairs(first, second):
    rows = first.shape[0] // 4
    return [value[i * rows : (i + 1) * rows] for value in (first, second) for i in range(4)]


def pick_rows(core, value):
    rows = value.shape[0] // 2
    return jnp.where(core == 0, value[:rows], value[rows:])


def hold(values, space=pltpu.VMEM):
    return [pltpu.with_memory_space_constraint(value, space) for value in values]


def stage_kernel(wanted, place_ref, *refs):
    count = len(refs) // 2

    @pl.when(place_ref[0] == wanted)
    def _():
        copies = [
            pltpu.make_async_copy(refs[k], refs[count + k], refs[-1].at[k]) for k in range(count)
        ]
        for copy in copies:
            copy.start()
        for copy in copies:
            copy.wait()


def stage(wanted, place, values):
    return pl.pallas_call(
        functools.partial(stage_kernel, wanted),
        out_shape=[pltpu.VMEM(value.shape, value.dtype) for value in values],
        in_specs=[pl.BlockSpec(memory_space=pltpu.SMEM)]
        + [pl.BlockSpec(memory_space=pltpu.HBM)] * len(values),
        out_specs=[pl.BlockSpec(memory_space=pltpu.VMEM)] * len(values),
        scratch_shapes=[pltpu.SemaphoreType.DMA((len(values),))],
        compiler_params=pltpu.CompilerParams(vmem_limit_bytes=STAGE_VMEM),
        cost_estimate=pl.CostEstimate(
            flops=0, bytes_accessed=4 * sum(value.size for value in values), transcendentals=0
        ),
    )(place, *hold(values, pltpu.HBM))


def call_inside(kernel, out_shapes, scalars, operands):
    inside = pl.BlockSpec(memory_space=pltpu.VMEM)
    return pl.pallas_call(
        kernel,
        out_shape=out_shapes,
        in_specs=[pl.BlockSpec(memory_space=pltpu.SMEM)] + [inside] * len(operands),
        out_specs=jax.tree.map(lambda out: inside, out_shapes),
        compiler_params=pltpu.CompilerParams(vmem_limit_bytes=KERNEL_VMEM),
    )(scalars, *hold(operands))


def front_kernel(place_ref, residual_hbm, gain_hbm, router_hbm, routes, out, *scratch):
    residual, gain, router, arrived = scratch
    copies = [
        pltpu.make_async_copy(source, target, arrived.at[k])
        for k, (source, target) in enumerate(
            ((residual_hbm, residual), (gain_hbm, gain), (router_hbm, router))
        )
    ]
    for copy in copies:
        copy.start()
    for copy in copies:
        copy.wait()
    core = place_ref[1]
    x_rows = pick_rows(core, residual[0].astype(F32))
    normed = x_rows * rms_scale(x_rows) * gain[...].astype(F32)
    logits = lax.dot_general(
        router[0].astype(F32),
        normed,
        (((1,), (1,)), ((), ())),
        precision=lax.Precision.HIGHEST,
        preferred_element_type=F32,
    )
    scores = 1.0 / (1.0 + jnp.exp(-logits))
    experts, rows = scores.shape
    chosen = routes[0]
    chosen = jnp.where(core == 0, chosen[:, :rows], chosen[:, rows:])
    expert_ids = lax.broadcasted_iota(jnp.int32, scores.shape, 0)
    named = jnp.zeros(scores.shape, F32)
    for k in range(chosen.shape[0]):
        named = jnp.where(chosen[k : k + 1] == expert_ids, 1.0, named)
    picked = named * scores
    weight = (ROUTE_SCALE * picked / jnp.sum(picked, axis=0, keepdims=True)).T
    width = normed.shape[1]
    spare = jnp.zeros((weight.shape[0], out.shape[1] - width - weight.shape[1]), F32)
    out[:, :width] = normed.astype(BF16)
    out[:, width:] = jnp.concatenate([weight, spare], axis=1).astype(BF16)


def front(place, residual, moe_gain, router, routes):
    shape = (residual.shape[1] // 2, residual.shape[2] + WEIGHT_LANES)
    anywhere = pl.BlockSpec(memory_space=pltpu.HBM)
    return pl.pallas_call(
        front_kernel,
        out_shape=jax.ShapeDtypeStruct(shape, BF16),
        in_specs=[pl.BlockSpec(memory_space=pltpu.SMEM)]
        + [anywhere] * 3
        + [pl.BlockSpec(memory_space=pltpu.VMEM)],
        out_specs=pl.BlockSpec(memory_space=pltpu.VMEM),
        scratch_shapes=[
            pltpu.VMEM(residual.shape, BF16),
            pltpu.VMEM(moe_gain.shape, BF16),
            pltpu.VMEM(router.shape, BF16),
            pltpu.SemaphoreType.DMA((3,)),
        ],
        compiler_params=pltpu.CompilerParams(vmem_limit_bytes=KERNEL_VMEM),
    )(place, *hold((residual, moe_gain, router), pltpu.HBM), jnp.swapaxes(routes, 1, 2))


def project_kernel(
    place_ref,
    residual,
    back_same,
    back_flip,
    gain_own,
    gain_other,
    proj_own,
    proj_other,
    kv_gain,
    cosine,
    sine,
    updated_out,
    fresh_out,
):
    core = place_ref[1]
    moe_out = back_same[...].astype(F32) + back_flip[...].astype(F32)
    updated = (pick_rows(core, residual[0].astype(F32)) + moe_out).astype(BF16)
    updated_out[...] = updated
    updated = updated.astype(F32)
    half = gain_own.shape[1]
    low, high = updated[:, :half], updated[:, half:]
    total = 0.0
    for part, gain, proj in (
        (jnp.where(core == 0, low, high), gain_own, proj_own),
        (jnp.where(core == 0, high, low), gain_other, proj_other),
    ):
        scaled = (part * gain[...].astype(F32)).astype(BF16)
        total = total + lax.dot_general(
            scaled, proj[...], (((1,), (1,)), ((), ())), preferred_element_type=F32
        )
    kv = total * rms_scale(updated)
    width = kv_gain.shape[1]
    latent, rope = kv[:, :width], kv[:, width:]
    turn = rope.shape[1] // 2
    a, c = rope[:, :turn], rope[:, turn:]
    fresh_out[:, :width] = (latent * rms_scale(latent) * kv_gain[...].astype(F32)).astype(BF16)
    fresh_out[:, width:] = jnp.concatenate(
        [a * cosine[...] - c * sine[...], a * sine[...] + c * cosine[...]], axis=1
    ).astype(BF16)


def merge_kernel(
    place_ref,
    fresh_own,
    fresh_other,
    updated_own,
    updated_other,
    mixed,
    peak,
    mass,
    query_rot,
    query_lat,
    resid_out,
    latent_out,
    rope_out,
    attn_out,
):
    role, core = place_ref[0], place_ref[1]

    def both(own, other):
        own, other = own[...].astype(F32), other[...].astype(F32)
        first = jnp.where(core == 0, own, other)
        second = jnp.where(core == 0, other, own)
        return jnp.concatenate([first, second], axis=0)

    @pl.when(role == 0)
    def _():
        resid_out[0] = both(updated_own, updated_other).astype(BF16)
        fresh = both(fresh_own, fresh_other)
        width = latent_out.shape[2]
        latent, rope = fresh[:, :width], fresh[:, width:]
        latent_out[0] = latent.astype(BF16)
        rope_out[0] = rope.astype(BF16)
        for t in range(latent.shape[0]):
            lat = latent[t : t + 1]
            own = jnp.sum(query_lat[0, t].astype(F32) * lat, axis=1, keepdims=True)
            own += jnp.sum(query_rot[t].astype(F32) * rope[t : t + 1], axis=1, keepdims=True)
            own *= SCORE_SCALE
            held = peak[t, :, :1]
            top = jnp.maximum(held, own)
            kept = jnp.exp(held - top)
            own = jnp.exp(own - top)
            total = mass[t, :, :1] * kept + own
            attn_out[0, t] = (mixed[t] * (kept / total) + (own / total) * lat).astype(BF16)

    @pl.when(role == 1)
    def _():
        for out in (resid_out, latent_out, rope_out, attn_out):
            out[...] = jnp.zeros_like(out)


def dot(left, right):
    return jnp.dot(left, right, preferred_element_type=F32)


def attend_cache(lengths, query_lat, query_rot, cache_lat, cache_rot, mixed, peak, mass, turned):
    heads, rope = turned.shape[1:]
    flat = heads * rope
    lane = lax.broadcasted_iota(jnp.int32, (heads, flat), 1)
    own_lanes = lane // rope == lax.broadcasted_iota(jnp.int32, (heads, flat), 0)
    fold = lax.broadcasted_iota(jnp.int32, (flat, rope), 0) % rope
    fold = (fold == lax.broadcasted_iota(jnp.int32, (flat, rope), 1)).astype(F32).astype(BF16)
    rotary = query_rot[...].astype(F32)
    for t in range(rotary.shape[0]):
        rot = dot(jnp.where(own_lanes, rotary[t : t + 1], 0.0).astype(BF16), fold).astype(BF16)
        turned[t] = rot
        scores = lax.dot_general(
            query_lat[t], cache_lat[t], (((1,), (1,)), ((), ())), preferred_element_type=F32
        )
        scores = (scores + dot(rot, cache_rot[t])) * SCORE_SCALE
        usable = lax.broadcasted_iota(jnp.int32, scores.shape, 1) < lengths[0, t]
        scores = jnp.where(usable, scores, -1e30)
        top = jnp.max(scores, axis=1, keepdims=True)
        weights = jnp.where(usable, jnp.exp(scores - top), 0.0)
        mixed[t] = dot(weights.astype(BF16), cache_lat[t])
        peak[t] = jnp.broadcast_to(top, peak.shape[1:])
        mass[t] = jnp.broadcast_to(jnp.sum(weights, axis=1, keepdims=True), mass.shape[1:])


def roles_kernel(place_ref, lengths, *refs):
    pieces, weights, far = refs[0:8], refs[8:14], refs[14:20]
    outs, cached, projections = refs[20:28], refs[28:32], refs[32:34]
    near, arrived = refs[34:38], refs[38]
    down_a, down_b = weights[4:]
    width, model_width = down_a.shape
    spans = [slice(start, start + CHUNK) for start in range(0, model_width, CHUNK)]

    @pl.when(place_ref[0] == 0)
    def _():
        sources = [far[k].at[0] for k in range(4)] + list(far[4:])
        copies = [
            pltpu.make_async_copy(source, target, arrived.at[k])
            for k, (source, target) in enumerate(zip(sources, (*near, *projections)))
        ]
        for copy in copies:
            copy.start()
        for copy in copies[:4]:
            copy.wait()
        attend_cache(lengths, *near, *cached)
        for copy in copies[4:]:
            copy.wait()

    @pl.when(place_ref[0] == 1)
    def _():
        sums = None
        for span in spans:
            rows = jnp.concatenate([piece[:, span] for piece in pieces], axis=0)
            parts = [dot(rows, weight[span, :]) for weight in weights[:4]]
            sums = parts if sums is None else [a + b for a, b in zip(sums, parts)]
        hidden = [
            (sums[k] / (1.0 + jnp.exp(-sums[k])) * sums[2 + k]).astype(BF16) for k in range(2)
        ]
        lanes = jnp.concatenate([piece[:, model_width:] for piece in pieces], axis=0).astype(F32)
        mine = lax.broadcasted_iota(jnp.int32, lanes.shape, 1) == place_ref[2]
        scale = jnp.sum(jnp.where(mine, lanes, 0.0), axis=1, keepdims=True)
        for span in spans:
            total = dot(hidden[0], down_a[:, span]) + dot(hidden[1], down_b[:, span])
            answer = (total * scale).astype(BF16)
            for k, out in enumerate(outs):
                size = out.shape[0]
                out[:, span] = answer[k * size : (k + 1) * size]


def roles(place, lengths, pieces, weights, attended, projections):
    model_width = weights[0].shape[0]
    _, tokens, heads, latent = attended[0].shape
    rope = attended[3].shape[2]
    smem = pl.BlockSpec(memory_space=pltpu.SMEM)
    inside = pl.BlockSpec(memory_space=pltpu.VMEM)
    anywhere = pl.BlockSpec(memory_space=pltpu.HBM)
    wide = jax.ShapeDtypeStruct((tokens, heads, WEIGHT_LANES), F32)
    results = pl.pallas_call(
        roles_kernel,
        out_shape=[jax.ShapeDtypeStruct((piece.shape[0], model_width), BF16) for piece in pieces]
        + [jax.ShapeDtypeStruct((tokens, heads, latent), F32), wide, wide]
        + [jax.ShapeDtypeStruct((tokens, heads, rope), BF16)]
        + [pltpu.VMEM(value.shape, value.dtype) for value in projections],
        in_specs=[smem, smem] + [inside] * 14 + [anywhere] * 6,
        out_specs=[inside] * 14,
        scratch_shapes=[pltpu.VMEM(value.shape[1:], BF16) for value in attended]
        + [pltpu.SemaphoreType.DMA((6,))],
        compiler_params=pltpu.CompilerParams(vmem_limit_bytes=ROLES_VMEM),
        cost_estimate=pl.CostEstimate(
            flops=3072 * model_width * weights[0].shape[1],
            bytes_accessed=12 * model_width * weights[0].shape[1],
            transcendentals=0,
        ),
    )(place, lengths, *hold(pieces), *hold(weights), *hold(attended, pltpu.HBM), *hold(projections, pltpu.HBM))
    return results[:8], results[8:12], results[12:]


def rms_scale(values):
    return lax.rsqrt(jnp.mean(values * values, axis=-1, keepdims=True) + NORM_EPS)


def turns(width, position):
    step_ids = lax.broadcasted_iota(jnp.int32, (1, width // 2), 1).astype(F32)
    inverse_freq = jnp.exp(-(2.0 * step_ids / width) * jnp.log(ROPE_BASE))
    angles = position.astype(F32)[:, None] * inverse_freq
    return jnp.cos(angles), jnp.sin(angles)


def body(
    residual,
    moe_gain,
    router,
    routes,
    gate_w,
    up_w,
    down_w,
    attn_gain,
    kv_proj,
    kv_gain,
    cache_latent,
    cache_rope,
    lengths,
    query_latent,
    query_rope,
):
    role = lax.axis_index("side").astype(jnp.int32)
    core = lax.axis_index("tp").astype(jnp.int32)
    own_expert = (lax.axis_index("grp") // NY).astype(jnp.int32)
    place = jnp.stack([role, core, own_expert])
    model_width = residual.shape[2]
    group_rows = residual.shape[1]
    rows = group_rows // 2
    latent_width = kv_gain.shape[1]
    rope_width = kv_proj.shape[1] - latent_width
    heads_here = query_latent.shape[2]
    barrier = lax.optimization_barrier

    gate_other, up_other = (send(value[0], other_core) for value in (gate_w, up_w))
    gain_other = send(attn_gain, other_core)

    outgoing = front(place, residual, moe_gain, router, routes)
    arrived = send(outgoing, across(0)), send(outgoing, across(1))
    gates = stage(1, place, (gate_w[0], up_w[0], down_w[0]))
    own_lengths = lax.dynamic_slice_in_dim(lengths[0], core * rows, rows, 0)
    cosine, sine = turns(rope_width, own_lengths)
    arrived, gates, gate_other, up_other, gain_other, cosine, sine, down_own = barrier(
        (arrived, gates, gate_other, up_other, gain_other, cosine, sine, down_w[0])
    )
    down_other = send(down_own, other_core)
    column = join_pairs(gather_ring(*arrived, 0)[:-1])
    column, down_other, kv_own = barrier((column, down_other, kv_proj[0]))
    kv_other = send(kv_own, other_core)
    others = stage(1, place, (gate_other, up_other, down_other))
    *pieces, others = gather_ring(*column, 1, others)

    answers, cached, projections = roles(
        place,
        lengths,
        pieces,
        (gates[0], others[0], gates[1], others[1], gates[2], others[2]),
        (query_latent, query_rope, cache_latent, cache_rope),
        (kv_own, kv_other),
    )
    back_same, back_flip = scatter_ring(split_pairs(*scatter_ring(answers, 1)), 0)
    back_same = send(back_same, across(0))
    back_flip = send(back_flip, across(1))

    updated, fresh = call_inside(
        project_kernel,
        [
            jax.ShapeDtypeStruct((rows, model_width), BF16),
            jax.ShapeDtypeStruct((rows, latent_width + rope_width), BF16),
        ],
        place,
        (
            residual,
            back_same,
            back_flip,
            attn_gain,
            gain_other,
            *projections,
            kv_gain,
            cosine,
            sine,
        ),
    )
    updated_other = send(updated, other_core)
    fresh_other = send(fresh, other_core)
    return call_inside(
        merge_kernel,
        [
            jax.ShapeDtypeStruct((1, group_rows, model_width), BF16),
            jax.ShapeDtypeStruct((1, group_rows, latent_width), BF16),
            jax.ShapeDtypeStruct((1, group_rows, rope_width), BF16),
            jax.ShapeDtypeStruct((1, group_rows, heads_here, latent_width), BF16),
        ],
        place,
        (fresh, fresh_other, updated, updated_other, *cached, query_latent),
    )


def solution(mesh):
    in_specs = (
        P("side", "grp", None),
        P("side", None),
        P("side", None, None),
        P("side", "grp", None),
        P("side", None, ("grp", "tp")),
        P("side", None, ("grp", "tp")),
        P("side", ("grp", "tp"), None),
        P("side", "tp"),
        P("side", None, "tp"),
        P("side", None),
        P("side", "grp", None, None),
        P("side", "grp", None, None),
        P("side", "grp"),
        P("side", "grp", "tp", None),
        P("side", "grp", "tp"),
    )
    out_specs = (
        P("side", "grp", None),
        P("side", "grp", None),
        P("side", "grp", None),
        P("side", "grp", "tp", None),
    )
    return jax.shard_map(body, mesh=mesh, in_specs=in_specs, out_specs=out_specs, check_vma=False)
```

```python
import functools

import jax
import jax.numpy as jnp
from jax import lax
from jax.experimental import pallas as pl
from jax.experimental.pallas import tpu as pltpu
from jax.sharding import PartitionSpec as P

NX = 4
NZ = 4
NY = 2
AXES = ("side", "grp", "tp")

NORM_EPS = 1e-06
ROUTE_SCALE = 2.5
ROPE_BASE = 10000.0
SCORE_SCALE = 192.0 ** (-0.5)
WEIGHT_LANES = 128
CHUNK = 1792
KERNEL_VMEM = 16 * 1024 * 1024
ROLES_VMEM = 16 * 1024 * 1024
STAGE_VMEM = 1024 * 1024

BF16 = jnp.bfloat16
F32 = jnp.float32


def pairs_of(partner):
    cells = [
        (side, x, z, y, t)
        for side in range(2)
        for x in range(NX)
        for z in range(NZ)
        for y in range(NY)
        for t in range(2)
    ]

    def place(cell):
        side, x, z, y, t = cell
        return (((side * NX + x) * NZ + z) * NY + y) * 2 + t

    return [(place(cell), place(partner(*cell))) for cell in cells]


def send(value, partner):
    return lax.ppermute(value, AXES, pairs_of(partner))


def across(flip):
    return lambda side, x, z, y, t: (1 - side, x, z, y ^ flip, t)


def other_core(side, x, z, y, t):
    return side, x, z, y, 1 - t


def ring(leg, flip):
    def partner(side, x, z, y, t):
        return (side, x ^ flip, z, y, t) if leg == t else (side, x, z ^ flip, y, t)

    return partner


def add(*values):
    total = values[0].astype(F32)
    for value in values[1:]:
        total = total + value.astype(F32)
    return total.astype(BF16)


def gather_ring(first, second, leg, beside=None):
    one_a = send(first, ring(leg, 1))
    three_b = send(second, ring(leg, 3))
    three_a = send(first, ring(leg, 3))
    one_b = send(second, ring(leg, 1))
    if beside is not None:
        one_a, three_b, beside = lax.optimization_barrier((one_a, three_b, beside))
    far_a = send(one_a, ring(leg, 3))
    far_b = send(three_b, ring(leg, 1))
    return first, second, one_a, one_b, three_a, three_b, far_a, far_b, beside


def scatter_ring(pieces, leg):
    first, second, one_a, one_b, three_a, three_b, far_a, far_b = pieces
    late_a = send(far_a, ring(leg, 3))
    late_b = send(far_b, ring(leg, 1))
    from_one_b = send(one_b, ring(leg, 1))
    from_three_a = send(three_a, ring(leg, 3))
    from_one_a = send(add(one_a, late_a), ring(leg, 1))
    from_three_b = send(add(three_b, late_b), ring(leg, 3))
    return add(first, from_one_a, from_three_a), add(second, from_one_b, from_three_b)


def join_pairs(values):
    half = len(values) // 2
    return jnp.concatenate(values[:half], axis=0), jnp.concatenate(values[half:], axis=0)


def split_pairs(first, second):
    rows = first.shape[0] // 4
    return [value[i * rows : (i + 1) * rows] for value in (first, second) for i in range(4)]


def pick_rows(core, value):
    rows = value.shape[0] // 2
    return jnp.where(core == 0, value[:rows], value[rows:])


def hold(values, space=pltpu.VMEM):
    return [pltpu.with_memory_space_constraint(value, space) for value in values]


def stage_kernel(wanted, place_ref, *refs):
    count = len(refs) // 2

    @pl.when(place_ref[0] == wanted)
    def _():
        copies = [
            pltpu.make_async_copy(refs[k], refs[count + k], refs[-1].at[k]) for k in range(count)
        ]
        for copy in copies:
            copy.start()
        for copy in copies:
            copy.wait()


def stage(wanted, place, values):
    return pl.pallas_call(
        functools.partial(stage_kernel, wanted),
        out_shape=[pltpu.VMEM(value.shape, value.dtype) for value in values],
        in_specs=[pl.BlockSpec(memory_space=pltpu.SMEM)]
        + [pl.BlockSpec(memory_space=pltpu.HBM)] * len(values),
        out_specs=[pl.BlockSpec(memory_space=pltpu.VMEM)] * len(values),
        scratch_shapes=[pltpu.SemaphoreType.DMA((len(values),))],
        compiler_params=pltpu.CompilerParams(vmem_limit_bytes=STAGE_VMEM),
        cost_estimate=pl.CostEstimate(
            flops=0, bytes_accessed=4 * sum(value.size for value in values), transcendentals=0
        ),
    )(place, *hold(values, pltpu.HBM))


def call_inside(kernel, out_shapes, scalars, operands):
    inside = pl.BlockSpec(memory_space=pltpu.VMEM)
    return pl.pallas_call(
        kernel,
        out_shape=out_shapes,
        in_specs=[pl.BlockSpec(memory_space=pltpu.SMEM)] + [inside] * len(operands),
        out_specs=jax.tree.map(lambda out: inside, out_shapes),
        compiler_params=pltpu.CompilerParams(vmem_limit_bytes=KERNEL_VMEM),
    )(scalars, *hold(operands))


def front_kernel(place_ref, residual_hbm, gain_hbm, router_hbm, routes, out, *scratch):
    residual, gain, router, arrived = scratch
    copies = [
        pltpu.make_async_copy(source, target, arrived.at[k])
        for k, (source, target) in enumerate(
            ((residual_hbm, residual), (gain_hbm, gain), (router_hbm, router))
        )
    ]
    for copy in copies:
        copy.start()
    for copy in copies:
        copy.wait()
    core = place_ref[1]
    x_rows = pick_rows(core, residual[0].astype(F32))
    normed = x_rows * rms_scale(x_rows) * gain[...].astype(F32)
    logits = lax.dot_general(
        router[0].astype(F32),
        normed,
        (((1,), (1,)), ((), ())),
        precision=lax.Precision.HIGHEST,
        preferred_element_type=F32,
    )
    scores = 1.0 / (1.0 + jnp.exp(-logits))
    experts, rows = scores.shape
    chosen = routes[0]
    chosen = jnp.where(core == 0, chosen[:, :rows], chosen[:, rows:])
    expert_ids = lax.broadcasted_iota(jnp.int32, scores.shape, 0)
    named = jnp.zeros(scores.shape, F32)
    for k in range(chosen.shape[0]):
        named = jnp.where(chosen[k : k + 1] == expert_ids, 1.0, named)
    picked = named * scores
    weight = (ROUTE_SCALE * picked / jnp.sum(picked, axis=0, keepdims=True)).T
    width = normed.shape[1]
    spare = jnp.zeros((weight.shape[0], out.shape[1] - width - weight.shape[1]), F32)
    out[:, :width] = normed.astype(BF16)
    out[:, width:] = jnp.concatenate([weight, spare], axis=1).astype(BF16)


def front(place, residual, moe_gain, router, routes):
    shape = (residual.shape[1] // 2, residual.shape[2] + WEIGHT_LANES)
    anywhere = pl.BlockSpec(memory_space=pltpu.HBM)
    return pl.pallas_call(
        front_kernel,
        out_shape=jax.ShapeDtypeStruct(shape, BF16),
        in_specs=[pl.BlockSpec(memory_space=pltpu.SMEM)]
        + [anywhere] * 3
        + [pl.BlockSpec(memory_space=pltpu.VMEM)],
        out_specs=pl.BlockSpec(memory_space=pltpu.VMEM),
        scratch_shapes=[
            pltpu.VMEM(residual.shape, BF16),
            pltpu.VMEM(moe_gain.shape, BF16),
            pltpu.VMEM(router.shape, BF16),
            pltpu.SemaphoreType.DMA((3,)),
        ],
        compiler_params=pltpu.CompilerParams(vmem_limit_bytes=KERNEL_VMEM),
    )(place, *hold((residual, moe_gain, router), pltpu.HBM), jnp.swapaxes(routes, 1, 2))


def project_kernel(
    place_ref,
    residual,
    back_flip,
    back_straight,
    gain_own,
    gain_other,
    proj_own,
    proj_other,
    kv_gain,
    cosine,
    sine,
    updated_out,
    fresh_out,
):
    core = place_ref[1]
    x_rows = pick_rows(core, residual[0].astype(F32))
    moe_out = back_flip[...].astype(F32) + back_straight[...].astype(F32)
    updated = (x_rows + moe_out).astype(BF16)
    updated_out[...] = updated
    updated = updated.astype(F32)
    half = gain_own.shape[1]
    low, high = updated[:, :half], updated[:, half:]
    total = 0.0
    for part, gain, proj in (
        (jnp.where(core == 0, low, high), gain_own, proj_own.at[0]),
        (jnp.where(core == 0, high, low), gain_other, proj_other),
    ):
        scaled = (part * gain[...].astype(F32)).astype(BF16)
        total = total + lax.dot_general(
            scaled, proj[...], (((1,), (1,)), ((), ())), preferred_element_type=F32
        )
    kv = total * rms_scale(updated)
    width = kv_gain.shape[1]
    latent, rope = kv[:, :width], kv[:, width:]
    turn = rope.shape[1] // 2
    a, c = rope[:, :turn], rope[:, turn:]
    cos, sin = pick_rows(core, cosine[...]), pick_rows(core, sine[...])
    fresh_out[:, :width] = (latent * rms_scale(latent) * kv_gain[...].astype(F32)).astype(BF16)
    fresh_out[:, width:] = jnp.concatenate(
        [a * cos - c * sin, a * sin + c * cos], axis=1
    ).astype(BF16)


def merge_kernel(
    place_ref,
    fresh_own,
    fresh_other,
    updated_own,
    updated_other,
    mixed,
    peak,
    mass,
    query_rot,
    query_lat,
    resid_out,
    latent_out,
    rope_out,
    attn_out,
):
    role, core = place_ref[0], place_ref[1]

    def both(own, other):
        own, other = own[...].astype(F32), other[...].astype(F32)
        first = jnp.where(core == 0, own, other)
        second = jnp.where(core == 0, other, own)
        return jnp.concatenate([first, second], axis=0)

    @pl.when(role == 0)
    def _():
        resid_out[0] = both(updated_own, updated_other).astype(BF16)
        fresh = both(fresh_own, fresh_other)
        width = latent_out.shape[2]
        latent, rope = fresh[:, :width], fresh[:, width:]
        latent_out[0] = latent.astype(BF16)
        rope_out[0] = rope.astype(BF16)
        for t in range(latent.shape[0]):
            lat = latent[t : t + 1]
            own = jnp.sum(query_lat[0, t].astype(F32) * lat, axis=1, keepdims=True)
            own += jnp.sum(query_rot[t].astype(F32) * rope[t : t + 1], axis=1, keepdims=True)
            own *= SCORE_SCALE
            held = peak[t, :, :1]
            top = jnp.maximum(held, own)
            kept = jnp.exp(held - top)
            own = jnp.exp(own - top)
            total = mass[t, :, :1] * kept + own
            attn_out[0, t] = (mixed[t] * (kept / total) + (own / total) * lat).astype(BF16)

    @pl.when(role == 1)
    def _():
        for out in (resid_out, latent_out, rope_out, attn_out):
            out[...] = jnp.zeros_like(out)


def dot(left, right):
    return jnp.dot(left, right, preferred_element_type=F32)


def attend_cache(lengths, query_lat, query_rot, cache_lat, cache_rot, mixed, peak, mass, turned):
    heads, rope = turned.shape[1:]
    flat = heads * rope
    lane = lax.broadcasted_iota(jnp.int32, (heads, flat), 1)
    own_lanes = lane // rope == lax.broadcasted_iota(jnp.int32, (heads, flat), 0)
    fold = lax.broadcasted_iota(jnp.int32, (flat, rope), 0) % rope
    fold = (fold == lax.broadcasted_iota(jnp.int32, (flat, rope), 1)).astype(F32).astype(BF16)
    rotary = query_rot[...].astype(F32)
    tokens = range(rotary.shape[0])
    spread = [jnp.where(own_lanes, rotary[t : t + 1], 0.0).astype(BF16) for t in tokens]
    folded = dot(jnp.concatenate(spread, axis=0), fold).astype(BF16)
    scores, usable = [], []
    for t in tokens:
        rot = folded[t * heads : (t + 1) * heads]
        turned[t] = rot
        latent_scores = lax.dot_general(
            query_lat[t], cache_lat[t], (((1,), (1,)), ((), ())), preferred_element_type=F32
        )
        scores.append(latent_scores + dot(rot, cache_rot[t]))
        slots = lax.broadcasted_iota(jnp.int32, scores[t].shape, 1)
        usable.append((slots < lengths[0, t]).astype(F32))
    usable = jnp.concatenate(usable, axis=0) > 0.0
    scores = jnp.where(usable, jnp.concatenate(scores, axis=0) * SCORE_SCALE, -1e30)
    top = jnp.max(scores, axis=1, keepdims=True)
    weights = jnp.where(usable, jnp.exp(scores - top), 0.0)
    total = jnp.sum(weights, axis=1, keepdims=True)
    weights = weights.astype(BF16)
    for t in tokens:
        own = slice(t * heads, (t + 1) * heads)
        mixed[t] = dot(weights[own], cache_lat[t])
        peak[t] = jnp.broadcast_to(top[own], peak.shape[1:])
        mass[t] = jnp.broadcast_to(total[own], mass.shape[1:])


def roles_kernel(place_ref, lengths, *refs):
    pieces, weights, far = refs[0:8], refs[8:14], refs[14:18]
    outs, cached = refs[18:26], refs[26:30]
    near, arrived = refs[30:34], refs[34]
    down_a, down_b = weights[4:]
    width, model_width = down_a.shape
    spans = [slice(start, start + CHUNK) for start in range(0, model_width, CHUNK)]

    @pl.when(place_ref[0] == 0)
    def _():
        copies = [
            pltpu.make_async_copy(source.at[0], target, arrived.at[k])
            for k, (source, target) in enumerate(zip(far, near))
        ]
        for copy in copies:
            copy.start()
        for copy in copies:
            copy.wait()
        attend_cache(lengths, *near, *cached)

    @pl.when(place_ref[0] == 1)
    def _():
        sums = None
        for span in spans:
            rows = jnp.concatenate([piece[:, span] for piece in pieces], axis=0)
            parts = [dot(rows, weight[span, :]) for weight in weights[:4]]
            sums = parts if sums is None else [a + b for a, b in zip(sums, parts)]
        hidden = [
            (sums[k] / (1.0 + jnp.exp(-sums[k])) * sums[2 + k]).astype(BF16) for k in range(2)
        ]
        lanes = jnp.concatenate([piece[:, model_width:] for piece in pieces], axis=0).astype(F32)
        mine = lax.broadcasted_iota(jnp.int32, lanes.shape, 1) == place_ref[2]
        scale = jnp.sum(jnp.where(mine, lanes, 0.0), axis=1, keepdims=True)
        for span in spans:
            total = dot(hidden[0], down_a[:, span]) + dot(hidden[1], down_b[:, span])
            answer = (total * scale).astype(BF16)
            for k, out in enumerate(outs):
                size = out.shape[0]
                out[:, span] = answer[k * size : (k + 1) * size]


def roles(place, lengths, pieces, weights, attended):
    model_width = weights[0].shape[0]
    _, tokens, heads, latent = attended[0].shape
    rope = attended[3].shape[2]
    smem = pl.BlockSpec(memory_space=pltpu.SMEM)
    inside = pl.BlockSpec(memory_space=pltpu.VMEM)
    anywhere = pl.BlockSpec(memory_space=pltpu.HBM)
    wide = jax.ShapeDtypeStruct((tokens, heads, WEIGHT_LANES), F32)
    results = pl.pallas_call(
        roles_kernel,
        out_shape=[jax.ShapeDtypeStruct((piece.shape[0], model_width), BF16) for piece in pieces]
        + [jax.ShapeDtypeStruct((tokens, heads, latent), F32), wide, wide]
        + [jax.ShapeDtypeStruct((tokens, heads, rope), BF16)],
        in_specs=[smem, smem] + [inside] * 14 + [anywhere] * 4,
        out_specs=[inside] * 12,
        scratch_shapes=[pltpu.VMEM(value.shape[1:], BF16) for value in attended]
        + [pltpu.SemaphoreType.DMA((4,))],
        compiler_params=pltpu.CompilerParams(vmem_limit_bytes=ROLES_VMEM),
        cost_estimate=pl.CostEstimate(
            flops=3072 * model_width * weights[0].shape[1],
            bytes_accessed=12 * model_width * weights[0].shape[1],
            transcendentals=0,
        ),
    )(place, lengths, *hold(pieces), *hold(weights), *hold(attended, pltpu.HBM))
    return results[:8], results[8:]


def rms_scale(values):
    return lax.rsqrt(jnp.mean(values * values, axis=-1, keepdims=True) + NORM_EPS)


def turns(width, position):
    step_ids = lax.broadcasted_iota(jnp.int32, (1, width // 2), 1).astype(F32)
    inverse_freq = jnp.exp(-(2.0 * step_ids / width) * jnp.log(ROPE_BASE))
    angles = position.astype(F32)[:, None] * inverse_freq
    return jnp.cos(angles), jnp.sin(angles)


def body(
    residual,
    moe_gain,
    router,
    routes,
    gate_w,
    up_w,
    down_w,
    attn_gain,
    kv_proj,
    kv_gain,
    cache_latent,
    cache_rope,
    lengths,
    query_latent,
    query_rope,
):
    role = lax.axis_index("side").astype(jnp.int32)
    core = lax.axis_index("tp").astype(jnp.int32)
    own_expert = (lax.axis_index("grp") // NY).astype(jnp.int32)
    place = jnp.stack([role, core, own_expert])
    model_width = residual.shape[2]
    group_rows = residual.shape[1]
    rows = group_rows // 2
    latent_width = kv_gain.shape[1]
    rope_width = kv_proj.shape[1] - latent_width
    heads_here = query_latent.shape[2]
    barrier = lax.optimization_barrier

    place, *swapped = barrier((place, gate_w[0], up_w[0], attn_gain))
    gate_other, up_other, gain_other = (send(value, other_core) for value in swapped)

    outgoing = front(place, residual, moe_gain, router, routes)
    flipped, straight = send(outgoing, across(1)), send(outgoing, across(0))
    gates = stage(1, place, (gate_w[0], up_w[0]))
    cosine, sine = turns(rope_width, lengths[0])
    flipped, straight, gates, cosine, sine, gain_other, gate_other, up_other, down_own = barrier(
        (flipped, straight, gates, cosine, sine, gain_other, gate_other, up_other, down_w[0])
    )
    down_other = send(down_own, other_core)
    column = join_pairs(gather_ring(flipped, straight, 0)[:-1])
    column, down_other, kv_own = barrier((column, down_other, kv_proj[0]))
    kv_other = send(kv_own, other_core)
    *pieces, downs = gather_ring(*column, 1, stage(1, place, (down_own,)))

    answers, cached = roles(
        place,
        lengths,
        pieces,
        (gates[0], gate_other, gates[1], up_other, downs[0], down_other),
        (query_latent, query_rope, cache_latent, cache_rope),
    )
    back_flip, back_straight = scatter_ring(split_pairs(*scatter_ring(answers, 1)), 0)
    back_flip = send(back_flip, across(1))
    back_straight = send(back_straight, across(0))

    updated, fresh = call_inside(
        project_kernel,
        [
            jax.ShapeDtypeStruct((rows, model_width), BF16),
            jax.ShapeDtypeStruct((rows, latent_width + rope_width), BF16),
        ],
        place,
        (
            residual,
            back_flip,
            back_straight,
            attn_gain,
            gain_other,
            kv_proj,
            kv_other,
            kv_gain,
            cosine,
            sine,
        ),
    )
    updated_other = send(updated, other_core)
    fresh_other = send(fresh, other_core)
    return call_inside(
        merge_kernel,
        [
            jax.ShapeDtypeStruct((1, group_rows, model_width), BF16),
            jax.ShapeDtypeStruct((1, group_rows, latent_width), BF16),
            jax.ShapeDtypeStruct((1, group_rows, rope_width), BF16),
            jax.ShapeDtypeStruct((1, group_rows, heads_here, latent_width), BF16),
        ],
        place,
        (fresh, fresh_other, updated, updated_other, *cached, query_latent),
    )


def solution(mesh):
    in_specs = (
        P("side", "grp", None),
        P("side", None),
        P("side", None, None),
        P("side", "grp", None),
        P("side", None, ("grp", "tp")),
        P("side", None, ("grp", "tp")),
        P("side", ("grp", "tp"), None),
        P("side", "tp"),
        P("side", None, "tp"),
        P("side", None),
        P("side", "grp", None, None),
        P("side", "grp", None, None),
        P("side", "grp"),
        P("side", "grp", "tp", None),
        P("side", "grp", "tp"),
    )
    out_specs = (
        P("side", "grp", None),
        P("side", "grp", None),
        P("side", "grp", None),
        P("side", "grp", "tp", None),
    )
    return jax.shard_map(body, mesh=mesh, in_specs=in_specs, out_specs=out_specs, check_vma=False)
```

```python
import functools

import jax
import jax.numpy as jnp
from jax import lax
from jax.experimental import pallas as pl
from jax.experimental.pallas import tpu as pltpu
from jax.sharding import PartitionSpec as P

NX = 4
NZ = 4
NY = 2
AXES = ("side", "grp", "tp")

NORM_EPS = 1e-06
ROUTE_SCALE = 2.5
ROPE_BASE = 10000.0
SCORE_SCALE = 192.0 ** (-0.5)
WEIGHT_LANES = 128
CHUNK = 1792
KERNEL_VMEM = 16 * 1024 * 1024
ROLES_VMEM = 16 * 1024 * 1024
STAGE_VMEM = 1024 * 1024

BF16 = jnp.bfloat16
F32 = jnp.float32


def pairs_of(partner):
    cells = [
        (side, x, z, y, t)
        for side in range(2)
        for x in range(NX)
        for z in range(NZ)
        for y in range(NY)
        for t in range(2)
    ]

    def place(cell):
        side, x, z, y, t = cell
        return (((side * NX + x) * NZ + z) * NY + y) * 2 + t

    return [(place(cell), place(partner(*cell))) for cell in cells]


def send(value, partner):
    return lax.ppermute(value, AXES, pairs_of(partner))


def across(flip):
    return lambda side, x, z, y, t: (1 - side, x, z, y ^ flip, t)


def other_core(side, x, z, y, t):
    return side, x, z, y, 1 - t


def ring(leg, flip):
    def partner(side, x, z, y, t):
        return (side, x ^ flip, z, y, t) if leg == t else (side, x, z ^ flip, y, t)

    return partner


def add(*values):
    total = values[0].astype(F32)
    for value in values[1:]:
        total = total + value.astype(F32)
    return total.astype(BF16)


def gather_ring(first, second, leg, beside=None):
    one_a = send(first, ring(leg, 1))
    three_b = send(second, ring(leg, 3))
    three_a = send(first, ring(leg, 3))
    one_b = send(second, ring(leg, 1))
    if beside is not None:
        one_a, three_b, beside = lax.optimization_barrier((one_a, three_b, beside))
    far_a = send(one_a, ring(leg, 3))
    far_b = send(three_b, ring(leg, 1))
    return first, second, one_a, one_b, three_a, three_b, far_a, far_b, beside


def scatter_ring(pieces, leg):
    first, second, one_a, one_b, three_a, three_b, far_a, far_b = pieces
    late_a = send(far_a, ring(leg, 3))
    late_b = send(far_b, ring(leg, 1))
    from_one_b = send(one_b, ring(leg, 1))
    from_three_a = send(three_a, ring(leg, 3))
    from_one_a = send(add(one_a, late_a), ring(leg, 1))
    from_three_b = send(add(three_b, late_b), ring(leg, 3))
    return add(first, from_one_a, from_three_a), add(second, from_one_b, from_three_b)


def join_pairs(values):
    half = len(values) // 2
    return jnp.concatenate(values[:half], axis=0), jnp.concatenate(values[half:], axis=0)


def split_pairs(first, second):
    rows = first.shape[0] // 4
    return [value[i * rows : (i + 1) * rows] for value in (first, second) for i in range(4)]


def pick_rows(core, value):
    rows = value.shape[0] // 2
    return jnp.where(core == 0, value[:rows], value[rows:])


def hold(values, space=pltpu.VMEM):
    return [pltpu.with_memory_space_constraint(value, space) for value in values]


def stage_kernel(wanted, place_ref, *refs):
    count = len(refs) // 2

    @pl.when(place_ref[0] == wanted)
    def _():
        copies = [
            pltpu.make_async_copy(refs[k], refs[count + k], refs[-1].at[k]) for k in range(count)
        ]
        for copy in copies:
            copy.start()
        for copy in copies:
            copy.wait()


def stage(wanted, place, values):
    return pl.pallas_call(
        functools.partial(stage_kernel, wanted),
        out_shape=[pltpu.VMEM(value.shape, value.dtype) for value in values],
        in_specs=[pl.BlockSpec(memory_space=pltpu.SMEM)]
        + [pl.BlockSpec(memory_space=pltpu.HBM)] * len(values),
        out_specs=[pl.BlockSpec(memory_space=pltpu.VMEM)] * len(values),
        scratch_shapes=[pltpu.SemaphoreType.DMA((len(values),))],
        compiler_params=pltpu.CompilerParams(vmem_limit_bytes=STAGE_VMEM),
        cost_estimate=pl.CostEstimate(
            flops=0, bytes_accessed=4 * sum(value.size for value in values), transcendentals=0
        ),
    )(place, *hold(values, pltpu.HBM))


def call_inside(kernel, out_shapes, scalars, operands):
    inside = pl.BlockSpec(memory_space=pltpu.VMEM)
    return pl.pallas_call(
        kernel,
        out_shape=out_shapes,
        in_specs=[pl.BlockSpec(memory_space=pltpu.SMEM)] + [inside] * len(operands),
        out_specs=jax.tree.map(lambda out: inside, out_shapes),
        compiler_params=pltpu.CompilerParams(vmem_limit_bytes=KERNEL_VMEM),
    )(scalars, *hold(operands))


def front_kernel(place_ref, residual_hbm, gain_hbm, router_hbm, routes_hbm, out, *scratch):
    residual, gain, router, routes, arrived = scratch
    copies = [
        pltpu.make_async_copy(source, target, arrived.at[k])
        for k, (source, target) in enumerate(
            ((residual_hbm, residual), (gain_hbm, gain), (router_hbm, router), (routes_hbm, routes))
        )
    ]
    for copy in copies:
        copy.start()
    for copy in copies:
        copy.wait()
    core = place_ref[1]
    x_rows = pick_rows(core, residual[0].astype(F32))
    normed = x_rows * rms_scale(x_rows) * gain[...].astype(F32)
    logits = lax.dot_general(
        router[0].astype(F32),
        normed,
        (((1,), (1,)), ((), ())),
        precision=lax.Precision.HIGHEST,
        preferred_element_type=F32,
    )
    scores = 1.0 / (1.0 + jnp.exp(-logits))
    experts, rows = scores.shape
    chosen = routes[0]
    chosen = jnp.where(core == 0, chosen[:, :rows], chosen[:, rows:])
    expert_ids = lax.broadcasted_iota(jnp.int32, scores.shape, 0)
    named = jnp.zeros(scores.shape, F32)
    for k in range(chosen.shape[0]):
        named = jnp.where(chosen[k : k + 1] == expert_ids, 1.0, named)
    picked = named * scores
    weight = (ROUTE_SCALE * picked / jnp.sum(picked, axis=0, keepdims=True)).T
    width = normed.shape[1]
    spare = jnp.zeros((weight.shape[0], out.shape[1] - width - weight.shape[1]), F32)
    out[:, :width] = normed.astype(BF16)
    out[:, width:] = jnp.concatenate([weight, spare], axis=1).astype(BF16)


def front(place, residual, moe_gain, router, routes):
    shape = (residual.shape[1] // 2, residual.shape[2] + WEIGHT_LANES)
    routes = jnp.swapaxes(routes, 1, 2)
    anywhere = pl.BlockSpec(memory_space=pltpu.HBM)
    return pl.pallas_call(
        front_kernel,
        out_shape=jax.ShapeDtypeStruct(shape, BF16),
        in_specs=[pl.BlockSpec(memory_space=pltpu.SMEM)]
        + [anywhere] * 4,
        out_specs=pl.BlockSpec(memory_space=pltpu.VMEM),
        scratch_shapes=[
            pltpu.VMEM(residual.shape, BF16),
            pltpu.VMEM(moe_gain.shape, BF16),
            pltpu.VMEM(router.shape, BF16),
            pltpu.VMEM(routes.shape, jnp.int32),
            pltpu.SemaphoreType.DMA((4,)),
        ],
        compiler_params=pltpu.CompilerParams(vmem_limit_bytes=KERNEL_VMEM),
    )(place, *hold((residual, moe_gain, router, routes), pltpu.HBM))


def project_kernel(
    place_ref,
    residual,
    back_flip,
    back_straight,
    gain_own,
    gain_other,
    proj_own,
    proj_other,
    kv_gain,
    cosine,
    sine,
    updated_out,
    fresh_out,
):
    core = place_ref[1]
    x_rows = pick_rows(core, residual[0].astype(F32))
    moe_out = back_flip[...].astype(F32) + back_straight[...].astype(F32)
    updated = (x_rows + moe_out).astype(BF16)
    updated_out[...] = updated
    updated = updated.astype(F32)
    half = gain_own.shape[1]
    low, high = updated[:, :half], updated[:, half:]
    total = 0.0
    for part, gain, proj in (
        (jnp.where(core == 0, low, high), gain_own, proj_own.at[0]),
        (jnp.where(core == 0, high, low), gain_other, proj_other),
    ):
        scaled = (part * gain[...].astype(F32)).astype(BF16)
        total = total + lax.dot_general(
            scaled, proj[...], (((1,), (1,)), ((), ())), preferred_element_type=F32
        )
    kv = total * rms_scale(updated)
    width = kv_gain.shape[1]
    latent, rope = kv[:, :width], kv[:, width:]
    turn = rope.shape[1] // 2
    a, c = rope[:, :turn], rope[:, turn:]
    cos, sin = pick_rows(core, cosine[...]), pick_rows(core, sine[...])
    fresh_out[:, :width] = (latent * rms_scale(latent) * kv_gain[...].astype(F32)).astype(BF16)
    fresh_out[:, width:] = jnp.concatenate(
        [a * cos - c * sin, a * sin + c * cos], axis=1
    ).astype(BF16)


def merge_kernel(
    place_ref,
    fresh_own,
    fresh_other,
    updated_own,
    updated_other,
    mixed,
    peak,
    mass,
    query_rot,
    query_lat,
    resid_out,
    latent_out,
    rope_out,
    attn_out,
):
    role, core = place_ref[0], place_ref[1]

    def both(own, other):
        own, other = own[...].astype(F32), other[...].astype(F32)
        first = jnp.where(core == 0, own, other)
        second = jnp.where(core == 0, other, own)
        return jnp.concatenate([first, second], axis=0)

    @pl.when(role == 0)
    def _():
        resid_out[0] = both(updated_own, updated_other).astype(BF16)
        fresh = both(fresh_own, fresh_other)
        width = latent_out.shape[2]
        latent, rope = fresh[:, :width], fresh[:, width:]
        latent_out[0] = latent.astype(BF16)
        rope_out[0] = rope.astype(BF16)
        for t in range(latent.shape[0]):
            lat = latent[t : t + 1]
            own = jnp.sum(query_lat[0, t].astype(F32) * lat, axis=1, keepdims=True)
            own += jnp.sum(query_rot[t].astype(F32) * rope[t : t + 1], axis=1, keepdims=True)
            own *= SCORE_SCALE
            held = peak[t, :, :1]
            top = jnp.maximum(held, own)
            kept = jnp.exp(held - top)
            own = jnp.exp(own - top)
            total = mass[t, :, :1] * kept + own
            attn_out[0, t] = (mixed[t] * (kept / total) + (own / total) * lat).astype(BF16)

    @pl.when(role == 1)
    def _():
        for out in (resid_out, latent_out, rope_out, attn_out):
            out[...] = jnp.zeros_like(out)


def dot(left, right):
    return jnp.dot(left, right, preferred_element_type=F32)


def attend_cache(lengths, query_lat, query_rot, cache_lat, cache_rot, mixed, peak, mass, turned):
    heads, rope = turned.shape[1:]
    flat = heads * rope
    lane = lax.broadcasted_iota(jnp.int32, (heads, flat), 1)
    own_lanes = lane // rope == lax.broadcasted_iota(jnp.int32, (heads, flat), 0)
    fold = lax.broadcasted_iota(jnp.int32, (flat, rope), 0) % rope
    fold = (fold == lax.broadcasted_iota(jnp.int32, (flat, rope), 1)).astype(F32).astype(BF16)
    rotary = query_rot[...].astype(F32)
    tokens = range(rotary.shape[0])
    spread = [jnp.where(own_lanes, rotary[t : t + 1], 0.0).astype(BF16) for t in tokens]
    folded = dot(jnp.concatenate(spread, axis=0), fold).astype(BF16)
    scores, usable = [], []
    for t in tokens:
        rot = folded[t * heads : (t + 1) * heads]
        turned[t] = rot
        latent_scores = lax.dot_general(
            query_lat[t], cache_lat[t], (((1,), (1,)), ((), ())), preferred_element_type=F32
        )
        scores.append(latent_scores + dot(rot, cache_rot[t]))
        slots = lax.broadcasted_iota(jnp.int32, scores[t].shape, 1)
        usable.append((slots < lengths[0, t]).astype(F32))
    usable = jnp.concatenate(usable, axis=0) > 0.0
    scores = jnp.where(usable, jnp.concatenate(scores, axis=0) * SCORE_SCALE, -1e30)
    top = jnp.max(scores, axis=1, keepdims=True)
    weights = jnp.where(usable, jnp.exp(scores - top), 0.0)
    total = jnp.sum(weights, axis=1, keepdims=True)
    weights = weights.astype(BF16)
    for t in tokens:
        own = slice(t * heads, (t + 1) * heads)
        mixed[t] = dot(weights[own], cache_lat[t])
        peak[t] = jnp.broadcast_to(top[own], peak.shape[1:])
        mass[t] = jnp.broadcast_to(total[own], mass.shape[1:])


def hidden_units(pieces, weights):
    sums = None
    for start in range(0, weights[0].shape[0], CHUNK):
        span = slice(start, start + CHUNK)
        rows = jnp.concatenate([piece[:, span] for piece in pieces], axis=0)
        parts = [dot(rows, weight[span, :]) for weight in weights]
        sums = parts if sums is None else [a + b for a, b in zip(sums, parts)]
    return [(sums[k] / (1.0 + jnp.exp(-sums[k])) * sums[2 + k]).astype(BF16) for k in range(2)]


def roles_kernel(place_ref, lengths, *refs):
    pieces, weights, far = refs[0:6], refs[6:10], refs[10:14]
    hidden, cached, near, arrived = refs[14], refs[15:19], refs[19:23], refs[23]
    width = weights[0].shape[1]

    @pl.when(place_ref[0] == 0)
    def _():
        copies = [
            pltpu.make_async_copy(source.at[0], target, arrived.at[k])
            for k, (source, target) in enumerate(zip(far, near))
        ]
        for copy in copies:
            copy.start()
        for copy in copies:
            copy.wait()
        attend_cache(lengths, *near, *cached)

    @pl.when(place_ref[0] == 1)
    def _():
        hidden[:, :width], hidden[:, width:] = hidden_units(pieces, weights)


def roles(place, lengths, pieces, weights, attended):
    model_width, width = weights[0].shape
    rows = sum(piece.shape[0] for piece in pieces)
    _, tokens, heads, latent = attended[0].shape
    rope = attended[3].shape[2]
    smem = pl.BlockSpec(memory_space=pltpu.SMEM)
    inside = pl.BlockSpec(memory_space=pltpu.VMEM)
    anywhere = pl.BlockSpec(memory_space=pltpu.HBM)
    wide = jax.ShapeDtypeStruct((tokens, heads, WEIGHT_LANES), F32)
    hidden, *cached = pl.pallas_call(
        roles_kernel,
        out_shape=[jax.ShapeDtypeStruct((rows, 2 * width), BF16)]
        + [jax.ShapeDtypeStruct((tokens, heads, latent), F32), wide, wide]
        + [jax.ShapeDtypeStruct((tokens, heads, rope), BF16)],
        in_specs=[smem, smem] + [inside] * 10 + [anywhere] * 4,
        out_specs=[inside] * 5,
        scratch_shapes=[pltpu.VMEM(value.shape[1:], BF16) for value in attended]
        + [pltpu.SemaphoreType.DMA((4,))],
        compiler_params=pltpu.CompilerParams(vmem_limit_bytes=ROLES_VMEM),
        cost_estimate=pl.CostEstimate(
            flops=8 * rows * model_width * width,
            bytes_accessed=8 * model_width * width,
            transcendentals=0,
        ),
    )(place, lengths, *hold(pieces), *hold(weights), *hold(attended, pltpu.HBM))
    return hidden, cached


def answer_kernel(place_ref, *refs):
    pieces, near, weights, outs = refs[0:8], refs[8], refs[9:15], refs[15:23]
    down_a, down_b = weights[4:]
    width, model_width = down_a.shape

    @pl.when(place_ref[0] == 1)
    def _():
        late = hidden_units(pieces[6:], weights[:4])
        early = near[:, :width], near[:, width:]
        hidden = [jnp.concatenate(parts, axis=0) for parts in zip(early, late)]
        lanes = jnp.concatenate([piece[:, model_width:] for piece in pieces], axis=0).astype(F32)
        mine = lax.broadcasted_iota(jnp.int32, lanes.shape, 1) == place_ref[2]
        scale = jnp.sum(jnp.where(mine, lanes, 0.0), axis=1, keepdims=True)
        for start in range(0, model_width, CHUNK):
            span = slice(start, start + CHUNK)
            total = dot(hidden[0], down_a[:, span]) + dot(hidden[1], down_b[:, span])
            answer = (total * scale).astype(BF16)
            for k, out in enumerate(outs):
                size = out.shape[0]
                out[:, span] = answer[k * size : (k + 1) * size]


def rms_scale(values):
    return lax.rsqrt(jnp.mean(values * values, axis=-1, keepdims=True) + NORM_EPS)


def turns(width, position):
    step_ids = lax.broadcasted_iota(jnp.int32, (1, width // 2), 1).astype(F32)
    inverse_freq = jnp.exp(-(2.0 * step_ids / width) * jnp.log(ROPE_BASE))
    angles = position.astype(F32)[:, None] * inverse_freq
    return jnp.cos(angles), jnp.sin(angles)


def body(
    residual,
    moe_gain,
    router,
    routes,
    gate_w,
    up_w,
    down_w,
    attn_gain,
    kv_proj,
    kv_gain,
    cache_latent,
    cache_rope,
    lengths,
    query_latent,
    query_rope,
):
    role = lax.axis_index("side").astype(jnp.int32)
    core = lax.axis_index("tp").astype(jnp.int32)
    own_expert = (lax.axis_index("grp") // NY).astype(jnp.int32)
    place = jnp.stack([role, core, own_expert])
    model_width = residual.shape[2]
    group_rows = residual.shape[1]
    rows = group_rows // 2
    latent_width = kv_gain.shape[1]
    rope_width = kv_proj.shape[1] - latent_width
    heads_here = query_latent.shape[2]
    barrier = lax.optimization_barrier

    place, *swapped = barrier((place, gate_w[0], up_w[0], attn_gain))
    gate_other, up_other, gain_other = (send(value, other_core) for value in swapped)

    outgoing = front(place, residual, moe_gain, router, routes)
    flipped, straight = send(outgoing, across(1)), send(outgoing, across(0))
    gates = stage(1, place, (gate_w[0], up_w[0]))
    cosine, sine = turns(rope_width, lengths[0])
    flipped, straight, gates, cosine, sine, gain_other, gate_other, up_other, down_own = barrier(
        (flipped, straight, gates, cosine, sine, gain_other, gate_other, up_other, down_w[0])
    )
    down_other = send(down_own, other_core)
    column = join_pairs(gather_ring(flipped, straight, 0)[:-1])
    column, down_other, kv_own = barrier((column, down_other, kv_proj[0]))
    kv_other = send(kv_own, other_core)
    *pieces, downs = gather_ring(*column, 1, stage(1, place, (down_own,)))

    gates = (gates[0], gate_other, gates[1], up_other)
    attended = (query_latent, query_rope, cache_latent, cache_rope)
    hidden, cached = roles(place, lengths, pieces[:6], gates, attended)
    answers = call_inside(
        answer_kernel,
        [jax.ShapeDtypeStruct((piece.shape[0], model_width), BF16) for piece in pieces],
        place,
        (*pieces, hidden, *gates, downs[0], down_other),
    )
    back_flip, back_straight = scatter_ring(split_pairs(*scatter_ring(answers, 1)), 0)
    back_flip = send(back_flip, across(1))
    back_straight = send(back_straight, across(0))

    updated, fresh = call_inside(
        project_kernel,
        [
            jax.ShapeDtypeStruct((rows, model_width), BF16),
            jax.ShapeDtypeStruct((rows, latent_width + rope_width), BF16),
        ],
        place,
        (
            residual,
            back_flip,
            back_straight,
            attn_gain,
            gain_other,
            kv_proj,
            kv_other,
            kv_gain,
            cosine,
            sine,
        ),
    )
    updated_other = send(updated, other_core)
    fresh_other = send(fresh, other_core)
    return call_inside(
        merge_kernel,
        [
            jax.ShapeDtypeStruct((1, group_rows, model_width), BF16),
            jax.ShapeDtypeStruct((1, group_rows, latent_width), BF16),
            jax.ShapeDtypeStruct((1, group_rows, rope_width), BF16),
            jax.ShapeDtypeStruct((1, group_rows, heads_here, latent_width), BF16),
        ],
        place,
        (fresh, fresh_other, updated, updated_other, *cached, query_latent),
    )


def solution(mesh):
    in_specs = (
        P("side", "grp", None),
        P("side", None),
        P("side", None, None),
        P("side", "grp", None),
        P("side", None, ("grp", "tp")),
        P("side", None, ("grp", "tp")),
        P("side", ("grp", "tp"), None),
        P("side", "tp"),
        P("side", None, "tp"),
        P("side", None),
        P("side", "grp", None, None),
        P("side", "grp", None, None),
        P("side", "grp"),
        P("side", "grp", "tp", None),
        P("side", "grp", "tp"),
    )
    out_specs = (
        P("side", "grp", None),
        P("side", "grp", None),
        P("side", "grp", None),
        P("side", "grp", "tp", None),
    )
    return jax.shard_map(body, mesh=mesh, in_specs=in_specs, out_specs=out_specs, check_vma=False)
```

```python
import functools

import jax
import jax.numpy as jnp
from jax import lax
from jax.experimental import pallas as pl
from jax.experimental.pallas import tpu as pltpu
from jax.sharding import PartitionSpec as P

NX = 4
NZ = 4
NY = 2
AXES = ("side", "grp", "tp")

NORM_EPS = 1e-06
ROUTE_SCALE = 2.5
ROPE_BASE = 10000.0
SCORE_SCALE = 192.0 ** (-0.5)
WEIGHT_LANES = 128
CHUNK = 1792
KERNEL_VMEM = 16 * 1024 * 1024
ROLES_VMEM = 16 * 1024 * 1024
STAGE_VMEM = 1024 * 1024

BF16 = jnp.bfloat16
F32 = jnp.float32


def pairs_of(partner):
    cells = [
        (side, x, z, y, t)
        for side in range(2)
        for x in range(NX)
        for z in range(NZ)
        for y in range(NY)
        for t in range(2)
    ]

    def place(cell):
        side, x, z, y, t = cell
        return (((side * NX + x) * NZ + z) * NY + y) * 2 + t

    return [(place(cell), place(partner(*cell))) for cell in cells]


def send(value, partner):
    return lax.ppermute(value, AXES, pairs_of(partner))


def across(flip):
    return lambda side, x, z, y, t: (1 - side, x, z, y ^ flip, t)


def other_core(side, x, z, y, t):
    return side, x, z, y, 1 - t


def ring(leg, flip):
    def partner(side, x, z, y, t):
        return (side, x ^ flip, z, y, t) if leg == t else (side, x, z ^ flip, y, t)

    return partner


def add(*values):
    total = values[0].astype(F32)
    for value in values[1:]:
        total = total + value.astype(F32)
    return total.astype(BF16)


def gather_ring(first, second, leg, beside=None):
    one_a = send(first, ring(leg, 1))
    three_b = send(second, ring(leg, 3))
    three_a = send(first, ring(leg, 3))
    one_b = send(second, ring(leg, 1))
    if beside is not None:
        one_a, three_b, beside = lax.optimization_barrier((one_a, three_b, beside))
    far_a = send(one_a, ring(leg, 3))
    far_b = send(three_b, ring(leg, 1))
    return first, second, one_a, one_b, three_a, three_b, far_a, far_b, beside


def scatter_ring(pieces, leg):
    first, second, one_a, one_b, three_a, three_b, far_a, far_b = pieces
    late_a = send(far_a, ring(leg, 3))
    late_b = send(far_b, ring(leg, 1))
    from_one_b = send(one_b, ring(leg, 1))
    from_three_a = send(three_a, ring(leg, 3))
    from_one_a = send(add(one_a, late_a), ring(leg, 1))
    from_three_b = send(add(three_b, late_b), ring(leg, 3))
    return add(first, from_one_a, from_three_a), add(second, from_one_b, from_three_b)


def join_pairs(values):
    half = len(values) // 2
    return jnp.concatenate(values[:half], axis=0), jnp.concatenate(values[half:], axis=0)


def split_pairs(first, second):
    rows = first.shape[0] // 4
    return [value[i * rows : (i + 1) * rows] for value in (first, second) for i in range(4)]


def pick_rows(core, value):
    rows = value.shape[0] // 2
    return jnp.where(core == 0, value[:rows], value[rows:])


def hold(values, space=pltpu.VMEM):
    return [pltpu.with_memory_space_constraint(value, space) for value in values]


def stage_kernel(wanted, place_ref, *refs):
    count = len(refs) // 2

    @pl.when(place_ref[0] == wanted)
    def _():
        copies = [
            pltpu.make_async_copy(refs[k], refs[count + k], refs[-1].at[k]) for k in range(count)
        ]
        for copy in copies:
            copy.start()
        for copy in copies:
            copy.wait()


def stage(wanted, place, values):
    return pl.pallas_call(
        functools.partial(stage_kernel, wanted),
        out_shape=[pltpu.VMEM(value.shape, value.dtype) for value in values],
        in_specs=[pl.BlockSpec(memory_space=pltpu.SMEM)]
        + [pl.BlockSpec(memory_space=pltpu.HBM)] * len(values),
        out_specs=[pl.BlockSpec(memory_space=pltpu.VMEM)] * len(values),
        scratch_shapes=[pltpu.SemaphoreType.DMA((len(values),))],
        compiler_params=pltpu.CompilerParams(vmem_limit_bytes=STAGE_VMEM),
        cost_estimate=pl.CostEstimate(
            flops=0, bytes_accessed=4 * sum(value.size for value in values), transcendentals=0
        ),
    )(place, *hold(values, pltpu.HBM))


def call_inside(kernel, out_shapes, scalars, operands):
    inside = pl.BlockSpec(memory_space=pltpu.VMEM)
    return pl.pallas_call(
        kernel,
        out_shape=out_shapes,
        in_specs=[pl.BlockSpec(memory_space=pltpu.SMEM)] + [inside] * len(operands),
        out_specs=jax.tree.map(lambda out: inside, out_shapes),
        compiler_params=pltpu.CompilerParams(vmem_limit_bytes=KERNEL_VMEM),
    )(scalars, *hold(operands))


def front_kernel(place_ref, residual_hbm, gain_hbm, router_hbm, routes_hbm, out, *scratch):
    residual, gain, router, routes, arrived = scratch
    copies = [
        pltpu.make_async_copy(source, target, arrived.at[k])
        for k, (source, target) in enumerate(
            ((residual_hbm, residual), (gain_hbm, gain), (router_hbm, router), (routes_hbm, routes))
        )
    ]
    for copy in copies:
        copy.start()
    for copy in copies:
        copy.wait()
    core = place_ref[1]
    x_rows = pick_rows(core, residual[0].astype(F32))
    normed = x_rows * rms_scale(x_rows) * gain[...].astype(F32)
    logits = lax.dot_general(
        router[0].astype(F32),
        normed,
        (((1,), (1,)), ((), ())),
        precision=lax.Precision.HIGHEST,
        preferred_element_type=F32,
    )
    scores = 1.0 / (1.0 + jnp.exp(-logits))
    experts, rows = scores.shape
    chosen = routes[0]
    chosen = jnp.where(core == 0, chosen[:, :rows], chosen[:, rows:])
    expert_ids = lax.broadcasted_iota(jnp.int32, scores.shape, 0)
    named = jnp.zeros(scores.shape, F32)
    for k in range(chosen.shape[0]):
        named = jnp.where(chosen[k : k + 1] == expert_ids, 1.0, named)
    picked = named * scores
    weight = (ROUTE_SCALE * picked / jnp.sum(picked, axis=0, keepdims=True)).T
    width = normed.shape[1]
    spare = jnp.zeros((weight.shape[0], out.shape[1] - width - weight.shape[1]), F32)
    out[:, :width] = normed.astype(BF16)
    out[:, width:] = jnp.concatenate([weight, spare], axis=1).astype(BF16)


def front(place, residual, moe_gain, router, routes):
    shape = (residual.shape[1] // 2, residual.shape[2] + WEIGHT_LANES)
    routes = jnp.swapaxes(routes, 1, 2)
    anywhere = pl.BlockSpec(memory_space=pltpu.HBM)
    return pl.pallas_call(
        front_kernel,
        out_shape=jax.ShapeDtypeStruct(shape, BF16),
        in_specs=[pl.BlockSpec(memory_space=pltpu.SMEM)]
        + [anywhere] * 4,
        out_specs=pl.BlockSpec(memory_space=pltpu.VMEM),
        scratch_shapes=[
            pltpu.VMEM(residual.shape, BF16),
            pltpu.VMEM(moe_gain.shape, BF16),
            pltpu.VMEM(router.shape, BF16),
            pltpu.VMEM(routes.shape, jnp.int32),
            pltpu.SemaphoreType.DMA((4,)),
        ],
        compiler_params=pltpu.CompilerParams(vmem_limit_bytes=KERNEL_VMEM),
    )(place, *hold((residual, moe_gain, router, routes), pltpu.HBM))


def project_kernel(
    place_ref,
    residual,
    back_flip,
    back_straight,
    gain_own,
    gain_other,
    proj_own,
    proj_other,
    kv_gain,
    cosine,
    sine,
    updated_out,
    fresh_out,
):
    core = place_ref[1]
    x_rows = pick_rows(core, residual[0].astype(F32))
    moe_out = back_flip[...].astype(F32) + back_straight[...].astype(F32)
    updated = (x_rows + moe_out).astype(BF16)
    updated_out[...] = updated
    updated = updated.astype(F32)
    half = gain_own.shape[1]
    low, high = updated[:, :half], updated[:, half:]
    total = 0.0
    for part, gain, proj in (
        (jnp.where(core == 0, low, high), gain_own, proj_own.at[0]),
        (jnp.where(core == 0, high, low), gain_other, proj_other),
    ):
        scaled = (part * gain[...].astype(F32)).astype(BF16)
        total = total + lax.dot_general(
            scaled, proj[...], (((1,), (1,)), ((), ())), preferred_element_type=F32
        )
    kv = total * rms_scale(updated)
    width = kv_gain.shape[1]
    latent, rope = kv[:, :width], kv[:, width:]
    turn = rope.shape[1] // 2
    a, c = rope[:, :turn], rope[:, turn:]
    cos, sin = pick_rows(core, cosine[...]), pick_rows(core, sine[...])
    fresh_out[:, :width] = (latent * rms_scale(latent) * kv_gain[...].astype(F32)).astype(BF16)
    fresh_out[:, width:] = jnp.concatenate(
        [a * cos - c * sin, a * sin + c * cos], axis=1
    ).astype(BF16)


def merge_kernel(
    place_ref,
    fresh_own,
    fresh_other,
    updated_own,
    updated_other,
    mixed,
    peak,
    mass,
    query_rot,
    query_lat,
    resid_out,
    latent_out,
    rope_out,
    attn_out,
):
    role, core = place_ref[0], place_ref[1]

    def both(own, other):
        own, other = own[...].astype(F32), other[...].astype(F32)
        first = jnp.where(core == 0, own, other)
        second = jnp.where(core == 0, other, own)
        return jnp.concatenate([first, second], axis=0)

    @pl.when(role == 0)
    def _():
        resid_out[0] = both(updated_own, updated_other).astype(BF16)
        fresh = both(fresh_own, fresh_other)
        width = latent_out.shape[2]
        latent, rope = fresh[:, :width], fresh[:, width:]
        latent_out[0] = latent.astype(BF16)
        rope_out[0] = rope.astype(BF16)
        for t in range(latent.shape[0]):
            lat = latent[t : t + 1]
            own = jnp.sum(query_lat[0, t].astype(F32) * lat, axis=1, keepdims=True)
            own += jnp.sum(query_rot[t].astype(F32) * rope[t : t + 1], axis=1, keepdims=True)
            own *= SCORE_SCALE
            held = peak[t, :, :1]
            top = jnp.maximum(held, own)
            kept = jnp.exp(held - top)
            own = jnp.exp(own - top)
            total = mass[t, :, :1] * kept + own
            attn_out[0, t] = (mixed[t] * (kept / total) + (own / total) * lat).astype(BF16)

    @pl.when(role == 1)
    def _():
        for out in (resid_out, latent_out, rope_out, attn_out):
            out[...] = jnp.zeros_like(out)


def dot(left, right):
    return jnp.dot(left, right, preferred_element_type=F32)


def attend_cache(lengths, query_lat, query_rot, cache_lat, cache_rot, mixed, peak, mass, turned):
    heads, rope = turned.shape[1:]
    flat = heads * rope
    lane = lax.broadcasted_iota(jnp.int32, (heads, flat), 1)
    own_lanes = lane // rope == lax.broadcasted_iota(jnp.int32, (heads, flat), 0)
    fold = lax.broadcasted_iota(jnp.int32, (flat, rope), 0) % rope
    fold = (fold == lax.broadcasted_iota(jnp.int32, (flat, rope), 1)).astype(F32).astype(BF16)
    rotary = query_rot[...].astype(F32)
    tokens = range(rotary.shape[0])
    spread = [jnp.where(own_lanes, rotary[t : t + 1], 0.0).astype(BF16) for t in tokens]
    folded = dot(jnp.concatenate(spread, axis=0), fold).astype(BF16)
    scores, usable = [], []
    for t in tokens:
        rot = folded[t * heads : (t + 1) * heads]
        turned[t] = rot
        latent_scores = lax.dot_general(
            query_lat[t], cache_lat[t], (((1,), (1,)), ((), ())), preferred_element_type=F32
        )
        scores.append(latent_scores + dot(rot, cache_rot[t]))
        slots = lax.broadcasted_iota(jnp.int32, scores[t].shape, 1)
        usable.append((slots < lengths[0, t]).astype(F32))
    usable = jnp.concatenate(usable, axis=0) > 0.0
    scores = jnp.where(usable, jnp.concatenate(scores, axis=0) * SCORE_SCALE, -1e30)
    top = jnp.max(scores, axis=1, keepdims=True)
    weights = jnp.where(usable, jnp.exp(scores - top), 0.0)
    total = jnp.sum(weights, axis=1, keepdims=True)
    weights = weights.astype(BF16)
    for t in tokens:
        own = slice(t * heads, (t + 1) * heads)
        mixed[t] = dot(weights[own], cache_lat[t])
        peak[t] = jnp.broadcast_to(top[own], peak.shape[1:])
        mass[t] = jnp.broadcast_to(total[own], mass.shape[1:])


def hidden_units(pieces, weights):
    sums = None
    for start in range(0, weights[0].shape[0], CHUNK):
        span = slice(start, start + CHUNK)
        rows = jnp.concatenate([piece[:, span] for piece in pieces], axis=0)
        parts = [dot(rows, weight[span, :]) for weight in weights]
        sums = parts if sums is None else [a + b for a, b in zip(sums, parts)]
    return [(sums[k] / (1.0 + jnp.exp(-sums[k])) * sums[2 + k]).astype(BF16) for k in range(2)]


def roles_kernel(place_ref, lengths, *refs):
    pieces, weights, far = refs[0:6], refs[6:10], refs[10:14]
    hidden, cached, near, arrived = refs[14], refs[15:19], refs[19:23], refs[23]
    width = weights[0].shape[1]

    @pl.when(place_ref[0] == 0)
    def _():
        copies = [
            pltpu.make_async_copy(source.at[0], target, arrived.at[k])
            for k, (source, target) in enumerate(zip(far, near))
        ]
        for copy in copies:
            copy.start()
        for copy in copies:
            copy.wait()
        attend_cache(lengths, *near, *cached)

    @pl.when(place_ref[0] == 1)
    def _():
        hidden[:, :width], hidden[:, width:] = hidden_units(pieces, weights)


def roles(place, lengths, pieces, weights, attended):
    model_width, width = weights[0].shape
    rows = sum(piece.shape[0] for piece in pieces)
    _, tokens, heads, latent = attended[0].shape
    rope = attended[3].shape[2]
    smem = pl.BlockSpec(memory_space=pltpu.SMEM)
    inside = pl.BlockSpec(memory_space=pltpu.VMEM)
    anywhere = pl.BlockSpec(memory_space=pltpu.HBM)
    wide = jax.ShapeDtypeStruct((tokens, heads, WEIGHT_LANES), F32)
    hidden, *cached = pl.pallas_call(
        roles_kernel,
        out_shape=[jax.ShapeDtypeStruct((rows, 2 * width), BF16)]
        + [jax.ShapeDtypeStruct((tokens, heads, latent), F32), wide, wide]
        + [jax.ShapeDtypeStruct((tokens, heads, rope), BF16)],
        in_specs=[smem, smem] + [inside] * 10 + [anywhere] * 4,
        out_specs=[inside] * 5,
        scratch_shapes=[pltpu.VMEM(value.shape[1:], BF16) for value in attended]
        + [pltpu.SemaphoreType.DMA((4,))],
        compiler_params=pltpu.CompilerParams(vmem_limit_bytes=ROLES_VMEM),
        cost_estimate=pl.CostEstimate(
            flops=8 * rows * model_width * width,
            bytes_accessed=8 * model_width * width,
            transcendentals=0,
        ),
    )(place, lengths, *hold(pieces), *hold(weights), *hold(attended, pltpu.HBM))
    return hidden, cached


def answer_kernel(place_ref, *refs):
    pieces, near, weights, outs = refs[0:8], refs[8], refs[9:15], refs[15:23]
    down_a, down_b = weights[4:]
    width, model_width = down_a.shape

    @pl.when(place_ref[0] == 1)
    def _():
        late = hidden_units(pieces[6:], weights[:4])
        early = near[:, :width], near[:, width:]
        hidden = [jnp.concatenate(parts, axis=0) for parts in zip(early, late)]
        lanes = jnp.concatenate([piece[:, model_width:] for piece in pieces], axis=0).astype(F32)
        mine = lax.broadcasted_iota(jnp.int32, lanes.shape, 1) == place_ref[2]
        scale = jnp.sum(jnp.where(mine, lanes, 0.0), axis=1, keepdims=True)
        for start in range(0, model_width, CHUNK):
            span = slice(start, start + CHUNK)
            total = dot(hidden[0], down_a[:, span]) + dot(hidden[1], down_b[:, span])
            answer = (total * scale).astype(BF16)
            for k, out in enumerate(outs):
                size = out.shape[0]
                out[:, span] = answer[k * size : (k + 1) * size]


def rms_scale(values):
    return lax.rsqrt(jnp.mean(values * values, axis=-1, keepdims=True) + NORM_EPS)


def turns(width, position):
    step_ids = lax.broadcasted_iota(jnp.int32, (1, width // 2), 1).astype(F32)
    inverse_freq = jnp.exp(-(2.0 * step_ids / width) * jnp.log(ROPE_BASE))
    angles = position.astype(F32)[:, None] * inverse_freq
    return jnp.cos(angles), jnp.sin(angles)


def body(
    residual,
    moe_gain,
    router,
    routes,
    gate_w,
    up_w,
    down_w,
    attn_gain,
    kv_proj,
    kv_gain,
    cache_latent,
    cache_rope,
    lengths,
    query_latent,
    query_rope,
):
    role = lax.axis_index("side").astype(jnp.int32)
    core = lax.axis_index("tp").astype(jnp.int32)
    own_expert = (lax.axis_index("grp") // NY).astype(jnp.int32)
    place = jnp.stack([role, core, own_expert])
    model_width = residual.shape[2]
    group_rows = residual.shape[1]
    rows = group_rows // 2
    latent_width = kv_gain.shape[1]
    rope_width = kv_proj.shape[1] - latent_width
    heads_here = query_latent.shape[2]
    barrier = lax.optimization_barrier

    place, *swapped = barrier((place, gate_w[0], up_w[0], attn_gain))
    gate_other, up_other, gain_other = (send(value, other_core) for value in swapped)

    outgoing = front(place, residual, moe_gain, router, routes)
    flipped, straight = send(outgoing, across(1)), send(outgoing, across(0))
    gates = stage(1, place, (gate_w[0], up_w[0]))
    cosine, sine = turns(rope_width, lengths[0])
    flipped, straight, gates, cosine, sine, gain_other, gate_other, up_other, down_own = barrier(
        (flipped, straight, gates, cosine, sine, gain_other, gate_other, up_other, down_w[0])
    )
    down_other = send(down_own, other_core)
    column = join_pairs(gather_ring(flipped, straight, 0)[:-1])
    column, down_other, kv_own = barrier((column, down_other, kv_proj[0]))
    kv_other = send(kv_own, other_core)
    *pieces, downs = gather_ring(*column, 1, stage(1, place, (down_own,)))

    gates = (gates[0], gate_other, gates[1], up_other)
    attended = (query_latent, query_rope, cache_latent, cache_rope)
    hidden, cached = roles(place, lengths, pieces[:6], gates, attended)
    hidden, kv_other = barrier((hidden, kv_other))
    answers = call_inside(
        answer_kernel,
        [jax.ShapeDtypeStruct((piece.shape[0], model_width), BF16) for piece in pieces],
        place,
        (*pieces, hidden, *gates, downs[0], down_other),
    )
    back_flip, back_straight = scatter_ring(split_pairs(*scatter_ring(answers, 1)), 0)
    back_flip = send(back_flip, across(1))
    back_straight = send(back_straight, across(0))

    updated, fresh = call_inside(
        project_kernel,
        [
            jax.ShapeDtypeStruct((rows, model_width), BF16),
            jax.ShapeDtypeStruct((rows, latent_width + rope_width), BF16),
        ],
        place,
        (
            residual,
            back_flip,
            back_straight,
            attn_gain,
            gain_other,
            kv_proj,
            kv_other,
            kv_gain,
            cosine,
            sine,
        ),
    )
    updated_other = send(updated, other_core)
    fresh_other = send(fresh, other_core)
    return call_inside(
        merge_kernel,
        [
            jax.ShapeDtypeStruct((1, group_rows, model_width), BF16),
            jax.ShapeDtypeStruct((1, group_rows, latent_width), BF16),
            jax.ShapeDtypeStruct((1, group_rows, rope_width), BF16),
            jax.ShapeDtypeStruct((1, group_rows, heads_here, latent_width), BF16),
        ],
        place,
        (fresh, fresh_other, updated, updated_other, *cached, query_latent),
    )


def solution(mesh):
    in_specs = (
        P("side", "grp", None),
        P("side", None),
        P("side", None, None),
        P("side", "grp", None),
        P("side", None, ("grp", "tp")),
        P("side", None, ("grp", "tp")),
        P("side", ("grp", "tp"), None),
        P("side", "tp"),
        P("side", None, "tp"),
        P("side", None),
        P("side", "grp", None, None),
        P("side", "grp", None, None),
        P("side", "grp"),
        P("side", "grp", "tp", None),
        P("side", "grp", "tp"),
    )
    out_specs = (
        P("side", "grp", None),
        P("side", "grp", None),
        P("side", "grp", None),
        P("side", "grp", "tp", None),
    )
    return jax.shard_map(body, mesh=mesh, in_specs=in_specs, out_specs=out_specs, check_vma=False)
```
